256 devices in a mesh: seq: 32 (over x, y, core), doc: 8 (over z).
Axes of the slice: x: 4, y: 4, z: 8, core: 2. Of those that a mesh axis runs over, the one named last changes fastest.
Arguments:
- q_self: bfloat16 [8, 4096, 4096], P('doc', 'seq'), may hold values from -6 to 6, as said below
- k_self: bfloat16 [8, 4096, 4096], P('doc', 'seq'), may hold values from -6 to 6, as said below
- v_self: bfloat16 [8, 4096, 4096], P('doc', 'seq'), may hold values from -6 to 6
- q_cross: bfloat16 [8, 4096, 4096], P('doc', 'seq'), may hold values from -6 to 6, as said below
- latents: bfloat16 [8, 32, 2, 64, 4096], P('doc', 'seq'), may hold values from -6 to 6, as said below
- media: int32 [8, 4096], P('doc', 'seq'), may hold values from -1 to 31, as said below
- gate: float32 [4096], replicated, may hold values from -1.2 to 1.2
- cotangent: bfloat16 [8, 4096, 4096], P('doc', 'seq'), may hold values from -6 to 6
Outputs:
- out: bfloat16 [8, 4096, 4096], P('doc', 'seq')
- grad_q_self: bfloat16 [8, 4096, 4096], P('doc', 'seq')
- grad_k_self: bfloat16 [8, 4096, 4096], P('doc', 'seq')
- grad_v_self: bfloat16 [8, 4096, 4096], P('doc', 'seq')
- grad_q_cross: bfloat16 [8, 4096, 4096], P('doc', 'seq')
- grad_latents: bfloat16 [8, 32, 2, 64, 4096], P('doc', 'seq')
- gate_grad: float32 [4096], replicated
The draws below stay inside these ranges and needn't reach their ends.
Inputs may be any that keep to these rules, and one draw needn't show every extreme that they name: `media`: each document uses its first 1 to 8 slots, placed at distinct positions of the document in slot order, and the last document of each sequence uses all 8; a token holds the slot of the last of them at or before it, or -1 if none, so values never fall within a document and stay inside its own slots. `q_self`: entries are of order one. `k_self`: entries are of order one. `q_cross`: entries are of order one. `latents`: entries are of order one.
All inputs are finite; a program needn't handle non-finite values.
Results may differ from the reference program's by a relative error of at most 0.01.
Values may be sent and summed in bfloat16 or wider, within the bound.
A program may use at most 128 MiB of HBM per device.

```python
import jax
import jax.numpy as jnp
from jax import lax

H = 32
E = 128
LAT = 64
MEDIA = 8
DOC_LEN = 1024
LENGTH = 4096
SEQS = 8
WIDTH = 4096
IMAGES = 32


def draw_q_self(key, part):
    key = jax.random.fold_in(key, 1)
    entries = jax.random.truncated_normal(key, -6.0, 6.0, (SEQS, LENGTH, WIDTH), jnp.float32)
    return entries.astype(jnp.bfloat16)


def draw_k_self(key, part):
    key = jax.random.fold_in(key, 2)
    entries = jax.random.truncated_normal(key, -6.0, 6.0, (SEQS, LENGTH, WIDTH), jnp.float32)
    return entries.astype(jnp.bfloat16)


def draw_q_cross(key, part):
    key = jax.random.fold_in(key, 3)
    entries = jax.random.truncated_normal(key, -6.0, 6.0, (SEQS, LENGTH, WIDTH), jnp.float32)
    return entries.astype(jnp.bfloat16)


def draw_latents(key, part):
    key = jax.random.fold_in(key, 4)
    shape = (SEQS, IMAGES, 2, LAT, WIDTH)
    entries = jax.random.truncated_normal(key, -6.0, 6.0, shape, jnp.float32)
    return entries.astype(jnp.bfloat16)


def draw_media(key, part):
    key = jax.random.fold_in(key, 11)
    doc_count = LENGTH // DOC_LEN
    key_list = jax.random.split(key, SEQS * doc_count)
    last_doc = jnp.arange(SEQS * doc_count) % doc_count == doc_count - 1

    def one_document(doc_key, is_last):
        count_key, place_key = jax.random.split(doc_key)
        image_count = jax.random.randint(count_key, (), 1, MEDIA + 1)
        image_count = jnp.where(is_last, MEDIA, image_count)
        image_place = jnp.sort(jax.random.permutation(place_key, DOC_LEN)[:MEDIA])
        places = jnp.arange(DOC_LEN)
        live = jnp.arange(MEDIA) < image_count
        seen_images = jnp.sum(((image_place[None, :] <= places[:, None]) & live[None, :]).astype(jnp.int32), axis=1)
        return seen_images
    seen_images = jax.vmap(one_document)(key_list, last_doc).reshape(SEQS, doc_count, DOC_LEN)
    slot_base = jnp.arange(doc_count)[None, :, None] * MEDIA
    media = jnp.where(seen_images > 0, slot_base + seen_images - 1, -1)
    return media.reshape(SEQS, LENGTH).astype(jnp.int32)


def shard_levels(key, shape, pieces, least, high):
    factor_of, own = 1.0, jax.random.fold_in(key, 6)
    for position, shards_of in pieces:
        heights = jnp.exp(jax.random.uniform(jax.random.fold_in(own, position), (shards_of,), jnp.float32, least / len(pieces), high / len(pieces)))
        factor_of = factor_of * jnp.repeat(heights, shape[position] // shards_of).reshape([-1 if axis == position else 1 for axis in range(len(shape))])
    return factor_of


def noise(own_key, extent, width, reach, shards=(), held_as=jnp.bfloat16):
    result = width * jax.random.normal(own_key, extent, jnp.float32)
    if shards:
        result = result * shard_levels(own_key, extent, shards, -0.22, 0.18)
    return jnp.clip(result, -reach, reach).astype(held_as)


def setup_inputs(seed: int = 0) -> dict:
    arg_keys = jax.random.split(jax.random.key(seed), 9)
    return {
        "q_self": draw_q_self(jax.random.fold_in(arg_keys[8], 71), 0),
        "k_self": draw_k_self(jax.random.fold_in(arg_keys[8], 71), 0),
        "v_self": noise(arg_keys[2], (SEQS, LENGTH, WIDTH), 1.0, 6.0, ((0, 8), (1, 32))),
        "q_cross": draw_q_cross(jax.random.fold_in(arg_keys[8], 71), 0),
        "latents": draw_latents(jax.random.fold_in(arg_keys[8], 71), 0),
        "media": draw_media(jax.random.fold_in(arg_keys[8], 71), 0),
        "gate": jnp.clip(jax.random.uniform(arg_keys[6], (WIDTH,), jnp.float32, -1.2, 1.2), -1.2, 1.2),
        "cotangent": noise(arg_keys[7], (SEQS, LENGTH, WIDTH), 1.0, 6.0, ((0, 8), (1, 32))),
    }


NEG_FILL = -1e30


def product(form, left, right):
    return jnp.einsum(form, lax.optimization_barrier(left).astype(jnp.float32), lax.optimization_barrier(right).astype(jnp.float32))


def self_document(inputs):
    query_rows, key_rows, value_rows, grad_rows = inputs
    factor = query_rows.shape[-1] ** -0.5
    score_full = factor * product("qhe,khe->hqk", query_rows, key_rows)
    places = jnp.arange(query_rows.shape[0], dtype=jnp.int32)
    causal = places[None, :] <= places[:, None]
    score_full = jnp.where(causal[None], score_full, -jnp.inf)
    weight_full = jnp.exp(score_full - jnp.max(score_full, axis=-1, keepdims=True))
    weight_full = weight_full / jnp.sum(weight_full, axis=-1, keepdims=True)
    weight_half = weight_full.astype(jnp.bfloat16)
    attended = product("hqk,khe->qhe", weight_half, value_rows)
    grad_values = product("hqk,qhe->khe", weight_half, grad_rows).astype(jnp.bfloat16)
    grad_weight = product("qhe,khe->hqk", grad_rows, value_rows)
    grad_score = weight_full * (grad_weight - jnp.sum(weight_full * grad_weight, axis=-1, keepdims=True))
    grad_score = grad_score.astype(jnp.bfloat16)
    grad_queries = (factor * product("hqk,khe->qhe", grad_score, key_rows)).astype(jnp.bfloat16)
    grad_keys = (factor * product("hqk,qhe->khe", grad_score, query_rows)).astype(jnp.bfloat16)
    return attended, grad_queries, grad_keys, grad_values


def cross_document(inputs, tanh_gate):
    query_rows, key_rows, value_rows, grad_rows, cited_slot = inputs
    factor = query_rows.shape[-1] ** -0.5
    score_full = factor * product("qhe,khe->hqk", query_rows, key_rows)
    owner_slot = jnp.arange(key_rows.shape[0], dtype=jnp.int32) // LAT
    allowed = owner_slot[None, :] == cited_slot[:, None]
    score_full = jnp.where(allowed[None], score_full, NEG_FILL)
    weight_full = jnp.exp(score_full - jnp.max(score_full, axis=-1, keepdims=True))
    weight_full = weight_full / jnp.sum(weight_full, axis=-1, keepdims=True)
    present = (cited_slot >= 0)[None, :, None]
    weight_full = jnp.where(present, weight_full, 0.0)
    weight_half = weight_full.astype(jnp.bfloat16)
    attended = product("hqk,khe->qhe", weight_half, value_rows)
    grad_gated = (grad_rows.astype(jnp.float32) * tanh_gate).astype(jnp.bfloat16)
    grad_values = product("hqk,qhe->khe", weight_half, grad_gated).astype(jnp.bfloat16)
    grad_weight = product("qhe,khe->hqk", grad_gated, value_rows)
    grad_score = weight_full * (grad_weight - jnp.sum(weight_full * grad_weight, axis=-1, keepdims=True))
    grad_score = grad_score.astype(jnp.bfloat16)
    grad_queries = (factor * product("hqk,khe->qhe", grad_score, key_rows)).astype(jnp.bfloat16)
    grad_keys = (factor * product("hqk,qhe->khe", grad_score, query_rows)).astype(jnp.bfloat16)
    gate_terms = jnp.sum(grad_rows.astype(jnp.float32) * attended, axis=0)
    return attended, grad_queries, grad_keys, grad_values, gate_terms


def reference(q_self, k_self, v_self, q_cross, latents, media, gate, cotangent):
    doc_count = LENGTH // DOC_LEN
    key_count = MEDIA * LAT
    tanh_all = jnp.tanh(gate).reshape(H, E)

    def one_sequence(inputs):
        query_seq, key_seq, value_seq, cross_seq, latent_seq, media_seq, grad_seq = inputs
        cited_slot = media_seq.reshape(doc_count, DOC_LEN)
        slot_base = MEDIA * jnp.arange(doc_count, dtype=jnp.int32)[:, None]
        cited_slot = jnp.where(cited_slot >= 0, cited_slot - slot_base, -1)

        def one_head(head_index):
            column_start = head_index * E

            def pick_head(tensor):
                return lax.dynamic_slice_in_dim(tensor, column_start, E, 1).reshape(doc_count, DOC_LEN, 1, E)

            latent_part = lax.dynamic_slice_in_dim(latent_seq, column_start, E, 3)
            key_parts = latent_part[:, 0].reshape(doc_count, key_count, 1, E)
            value_parts = latent_part[:, 1].reshape(doc_count, key_count, 1, E)
            tanh_gate = lax.dynamic_slice_in_dim(tanh_all, head_index, 1, 0)
            self_parts = lax.map(self_document, (pick_head(query_seq), pick_head(key_seq), pick_head(value_seq), pick_head(grad_seq)))
            cross_parts = lax.map(lambda doc_inputs: cross_document(doc_inputs, tanh_gate), (pick_head(cross_seq), key_parts, value_parts, pick_head(grad_seq), cited_slot))
            mixed_heads = (self_parts[0] + tanh_gate * cross_parts[0]).astype(jnp.bfloat16)
            latent_grad = jnp.stack([cross_parts[2].reshape(doc_count * MEDIA, LAT, E), cross_parts[3].reshape(doc_count * MEDIA, LAT, E)], axis=1)
            gate_part = (jnp.sum(cross_parts[4], axis=0) * (1.0 - tanh_gate * tanh_gate))[0]

            def to_rows(tensor):
                return tensor.reshape(LENGTH, E)

            return (to_rows(mixed_heads), to_rows(self_parts[1]), to_rows(self_parts[2]), to_rows(self_parts[3]), to_rows(cross_parts[1]), latent_grad, gate_part)

        results = lax.map(one_head, jnp.arange(H, dtype=jnp.int32))

        def to_columns(tensor):
            return tensor.transpose(1, 0, 2).reshape(LENGTH, WIDTH)

        latent_all = results[5].transpose(1, 2, 3, 0, 4).reshape(IMAGES, 2, LAT, WIDTH)
        return (to_columns(results[0]), to_columns(results[1]), to_columns(results[2]), to_columns(results[3]), to_columns(results[4]), latent_all, results[6].reshape(WIDTH))

    per_sequence = lax.map(one_sequence, (q_self, k_self, v_self, q_cross, latents, media, cotangent))
    gate_grad = jnp.sum(per_sequence[6], axis=0)
    return (per_sequence[0], per_sequence[1], per_sequence[2], per_sequence[3], per_sequence[4], per_sequence[5], gate_grad)
```

```python
import functools

import jax
import jax.numpy as jnp
from jax import lax
from jax.experimental import pallas as pl
from jax.experimental.pallas import tpu as pltpu
from jax.sharding import PartitionSpec as P

E = 128
LAT = 64
GROUP = 8
ROWS = 128
DOC = GROUP * ROWS
HEADS = 4
COLS = HEADS * E
KEYS = GROUP * LAT
BLOCK = 256
WIDTH = GROUP * COLS
SCALE = E**-0.5
NEG_FILL = -1e30
MESH = pl.DeviceIdType.MESH
F32 = jnp.float32
BF16 = jnp.bfloat16


def dot(left, right, left_dim, right_dim):
    return lax.dot_general(
        left, right, (((left_dim,), (right_dim,)), ((), ())), preferred_element_type=F32
    )


def softmax_and_grad(scores, weights_grad_of, inverse_of):
    peak = jnp.max(scores, axis=0, keepdims=True)
    weights = jnp.exp(SCALE * (scores - peak))
    weights = weights * inverse_of(jnp.sum(weights, axis=0, keepdims=True))
    half = weights.astype(BF16)
    weights_grad = weights_grad_of()
    inner = jnp.sum(weights * weights_grad, axis=0, keepdims=True)
    return half, (weights * (weights_grad - inner)).astype(BF16)


def cross_head(head, gate_row, media_row, qc_buf, cot_buf, lat_buf, mixed, gqc_buf, glat_buf, acc_k, acc_v):
    cols = pl.ds(pl.multiple_of(head * E, E), E)
    keys = lat_buf[:, 0, :, cols].reshape(KEYS, E)
    values = lat_buf[:, 1, :, cols].reshape(KEYS, E)
    tanh_gate = jnp.tanh(gate_row)
    slot = lax.broadcasted_iota(jnp.int32, (KEYS, BLOCK), 0) // LAT
    acc_k[pl.ds(0, KEYS), :] = jnp.zeros((KEYS, E), F32)
    acc_v[pl.ds(0, KEYS), :] = jnp.zeros((KEYS, E), F32)

    def step(i, gate_sum):
        rows = pl.ds(pl.multiple_of(i * BLOCK, BLOCK), BLOCK)
        cited = media_row(i)
        queries = qc_buf[rows, cols]
        cot = cot_buf[rows, cols].astype(F32)
        cot_cross = (cot * tanh_gate).astype(BF16)
        scores = dot(keys, queries, 1, 1)
        scores = jnp.where(slot == cited, scores, NEG_FILL)
        half, scores_grad = softmax_and_grad(
            scores,
            lambda: dot(values, cot_cross, 1, 1),
            lambda total: jnp.where(cited >= 0, 1.0 / total, 0.0),
        )
        out = dot(values, half, 0, 0).T
        mixed[rows, cols] = tanh_gate * out
        acc_v[pl.ds(0, KEYS), :] += dot(half, cot_cross, 1, 0)
        gqc_buf[rows, cols] = (SCALE * dot(keys, scores_grad, 0, 0)).T.astype(BF16)
        acc_k[pl.ds(0, KEYS), :] += dot(scores_grad, queries, 1, 0)
        return gate_sum + jnp.sum(cot * out, axis=0, keepdims=True)

    gate_sum = lax.fori_loop(0, DOC // BLOCK, step, jnp.zeros((1, E), F32))
    glat_buf[:, 0, :, cols] = (SCALE * acc_k[pl.ds(0, KEYS), :]).astype(BF16).reshape(GROUP, LAT, E)
    glat_buf[:, 1, :, cols] = acc_v[pl.ds(0, KEYS), :].astype(BF16).reshape(GROUP, LAT, E)
    return gate_sum * (1.0 - tanh_gate * tanh_gate)


def self_head(head, q_buf, k_buf, v_buf, cot_buf, mixed, out_buf, gq_buf, gk_buf, gv_buf, acc_k, acc_v):
    cols = pl.ds(pl.multiple_of(head * E, E), E)
    acc_k[...] = jnp.zeros((DOC, E), F32)
    acc_v[...] = jnp.zeros((DOC, E), F32)
    for i in range(DOC // BLOCK):
        rows = pl.ds(i * BLOCK, BLOCK)
        seen = pl.ds(0, (i + 1) * BLOCK)
        queries = q_buf[rows, cols]
        cot = cot_buf[rows, cols]
        keys = k_buf[seen, cols]
        values = v_buf[seen, cols]
        scores = dot(keys, queries, 1, 1)
        shape = scores.shape
        causal = lax.broadcasted_iota(jnp.int32, shape, 0) <= i * BLOCK + lax.broadcasted_iota(jnp.int32, shape, 1)
        scores = jnp.where(causal, scores, -jnp.inf)
        half, scores_grad = softmax_and_grad(
            scores, lambda: dot(values, cot, 1, 1), lambda total: 1.0 / total
        )
        out = dot(values, half, 0, 0).T
        out_buf[rows, cols] = (out + mixed[rows, cols]).astype(BF16)
        acc_v[seen, :] += dot(half, cot, 1, 0)
        gq_buf[rows, cols] = (SCALE * dot(keys, scores_grad, 0, 0)).T.astype(BF16)
        acc_k[seen, :] += dot(scores_grad, queries, 1, 0)
    gk_buf[:, cols] = (SCALE * acc_k[...]).astype(BF16)
    gv_buf[:, cols] = acc_v[...].astype(BF16)


def kernel(
    x_count, z_count,
    q_ref, k_ref, v_ref, qc_ref, lat_ref, cot_ref, media_ref, gate_ref,
    out_ref, gq_ref, gk_ref, gv_ref, gqc_ref, glat_ref, gate_out_ref,
    q_buf, k_buf, v_buf, qc_buf, cot_buf, lat_buf, media_buf,
    out_buf, gq_buf, gk_buf, gv_buf, gqc_buf, glat_buf,
    mixed, acc_k, acc_v, gate_own, gate_x, gate_z, gate_all,
    in_send, in_recv, out_send, out_recv, gx_send, gx_recv, gz_send, gz_recv, gg_send, gg_recv,
):
    seq = lax.axis_index("seq")
    doc = lax.axis_index("doc")
    x = seq // GROUP
    me = lax.rem(seq, GROUP)

    def in_group(k):
        rank = lax.rem(me + k, GROUP)
        return rank, {"seq": x * GROUP + rank}

    def along_x(k):
        return {"seq": lax.rem(x + k, x_count) * GROUP + me}

    def along_z(k):
        return {"doc": lax.rem(doc + k, z_count)}

    barrier = pltpu.get_barrier_semaphore()

    def greet(device):
        pl.semaphore_signal(barrier, inc=1, device_id=device, device_id_type=MESH)

    def greet_group(k, c):
        greet(in_group(k)[1])
        return c

    def greet_z(k, c):
        greet(along_z(k))
        return c

    def greet_x(k, c):
        greet(along_x(k))
        return c

    lax.fori_loop(1, GROUP, greet_group, 0)
    lax.fori_loop(1, x_count, greet_x, 0)
    lax.fori_loop(1, z_count, greet_z, 0)
    pl.semaphore_wait(barrier, GROUP - 1 + x_count - 1 + z_count - 1)

    own_rows = pl.ds(pl.multiple_of(me * ROWS, ROWS), ROWS)
    own_cols = pl.ds(pl.multiple_of(me * COLS, COLS), COLS)

    def in_views(t, rank):
        cols = pl.ds(pl.multiple_of(rank * COLS, COLS), COLS)
        if t == 0:
            return media_ref, media_buf.at[me]
        if t == 1:
            return lat_ref.at[0, 0, :, :, cols], lat_buf.at[me]
        ref, buf = {2: (cot_ref, cot_buf), 3: (qc_ref, qc_buf), 4: (k_ref, k_buf), 5: (q_ref, q_buf), 6: (v_ref, v_buf)}[t]
        return ref.at[0, :, cols], buf.at[own_rows]

    for part in ((0, 1, 2, 3), (4, 5, 6)):
        for t in part:
            src, dst = in_views(t, me)
            pltpu.make_async_copy(src, dst, in_recv.at[t]).start()

        def send(k, c, part=part):
            rank, device = in_group(k)
            for t in part:
                src, dst = in_views(t, rank)
                pltpu.make_async_remote_copy(
                    src_ref=src, dst_ref=dst, send_sem=in_send.at[t], recv_sem=in_recv.at[t],
                    device_id=device, device_id_type=MESH,
                ).start()
            return c

        lax.fori_loop(1, GROUP, send, 0)

    def await_bytes(ref, sem):
        pltpu.make_async_copy(ref, ref, sem).wait()

    in_bufs = (media_buf, lat_buf, cot_buf, qc_buf, k_buf, q_buf, v_buf)

    def out_views(t, head, rank):
        there = pl.ds(pl.multiple_of(me * COLS + head * E, E), E)
        here = pl.ds(pl.multiple_of(head * E, E), E)
        if t == 5:
            return glat_buf.at[rank, :, :, here], glat_ref.at[0, 0, :, :, there]
        ref, buf = ((out_ref, out_buf), (gq_ref, gq_buf), (gk_ref, gk_buf), (gv_ref, gv_buf), (gqc_ref, gqc_buf))[t]
        return buf.at[pl.ds(pl.multiple_of(rank * ROWS, ROWS), ROWS), here], ref.at[0, :, there]

    def send_out(head, part):
        for t in part:
            src, dst = out_views(t, head, me)
            pltpu.make_async_copy(src, dst, out_recv.at[t, head]).start()

        def send(k, c):
            rank, device = in_group(k)
            for t in part:
                src, dst = out_views(t, head, rank)
                pltpu.make_async_remote_copy(
                    src_ref=src, dst_ref=dst, send_sem=out_send.at[t, head], recv_sem=out_recv.at[t, head],
                    device_id=device, device_id_type=MESH,
                ).start()
            return c

        lax.fori_loop(1, GROUP, send, 0)

    for t in (0, 1, 2, 3):
        await_bytes(in_bufs[t], in_recv.at[t])
    first_slot = x * GROUP

    def media_row(i):
        pair = jnp.concatenate([media_buf[2 * i], media_buf[2 * i + 1]], axis=1)
        return jnp.where(pair >= 0, pair - first_slot, -1)

    def cross_step(head, c):
        gate_row = gate_ref[pl.ds(me * HEADS + head, 1), :]
        gate_own[pl.ds(head, 1), :] = cross_head(
            head, gate_row, media_row, qc_buf, cot_buf, lat_buf, mixed, gqc_buf, glat_buf, acc_k, acc_v
        )
        send_out(head, (4, 5))
        return c

    lax.fori_loop(0, HEADS, cross_step, 0)

    gate_x[x] = gate_own[...]

    def send_x(k, c):
        pltpu.make_async_remote_copy(
            src_ref=gate_own, dst_ref=gate_x.at[x], send_sem=gx_send.at[k], recv_sem=gx_recv.at[k],
            device_id=along_x(k), device_id_type=MESH,
        ).start()
        return c

    lax.fori_loop(1, x_count, send_x, 0)

    for t in (4, 5, 6):
        await_bytes(in_bufs[t], in_recv.at[t])

    def self_step(head, c):
        self_head(head, q_buf, k_buf, v_buf, cot_buf, mixed, out_buf, gq_buf, gk_buf, gv_buf, acc_k, acc_v)
        send_out(head, (0, 1, 2, 3))
        return c

    lax.fori_loop(0, HEADS, self_step, 0)

    def wait_x(k, c):
        pltpu.make_async_remote_copy(
            src_ref=gate_own, dst_ref=gate_x.at[x], send_sem=gx_send.at[k], recv_sem=gx_recv.at[k],
            device_id=along_x(k), device_id_type=MESH,
        ).wait()
        return c

    lax.fori_loop(1, x_count, wait_x, 0)
    gate_own[...] = jnp.sum(gate_x[...], axis=0)
    gate_z[doc] = gate_own[...]

    def copy_z(k):
        return pltpu.make_async_remote_copy(
            src_ref=gate_own, dst_ref=gate_z.at[doc], send_sem=gz_send.at[k], recv_sem=gz_recv.at[k],
            device_id=along_z(k), device_id_type=MESH,
        )

    def send_z(k, c):
        copy_z(k).start()
        return c

    def wait_z(k, c):
        copy_z(k).wait()
        return c

    lax.fori_loop(1, z_count, send_z, 0)
    lax.fori_loop(1, z_count, wait_z, 0)
    gate_own[...] = jnp.sum(gate_z[...], axis=0)
    gate_all[me] = gate_own[...]

    def copy_group(k):
        return pltpu.make_async_remote_copy(
            src_ref=gate_own, dst_ref=gate_all.at[me], send_sem=gg_send.at[k], recv_sem=gg_recv.at[k],
            device_id=in_group(k)[1], device_id_type=MESH,
        )

    def send_group(k, c):
        copy_group(k).start()
        return c

    def wait_group(k, c):
        copy_group(k).wait()
        return c

    lax.fori_loop(1, GROUP, send_group, 0)
    lax.fori_loop(1, GROUP, wait_group, 0)
    for rank in range(GROUP):
        gate_out_ref[pl.ds(rank * HEADS, HEADS), :] = gate_all[rank, pl.ds(0, HEADS), :]

    most = GROUP - 1
    for t, buf in enumerate(in_bufs):
        await_bytes(buf.at[pl.ds(0, most * (buf.shape[0] // GROUP))], in_send.at[t])

    def end(head, c):
        here = pl.ds(pl.multiple_of(head * E, E), E)
        for t, buf in enumerate((out_buf, gq_buf, gk_buf, gv_buf, gqc_buf)):
            await_bytes(buf.at[pl.ds(0, most * ROWS), here], out_send.at[t, head])
            await_bytes(buf.at[:, here], out_recv.at[t, head])
        await_bytes(glat_buf.at[pl.ds(0, most), :, :, here], out_send.at[5, head])
        await_bytes(glat_buf.at[:, :, :, here], out_recv.at[5, head])
        return c

    lax.fori_loop(0, HEADS, end, 0)


def finish_kernel(*refs):
    count = len(refs) // 2
    sems = refs[-1]
    copies = [pltpu.make_async_copy(refs[i], refs[count + i], sems.at[i]) for i in range(count)]
    for copy in copies:
        copy.start()
    for copy in copies:
        copy.wait()


def per_device(x_count, z_count, q, k, v, qc, lat, media, gate, cot):
    any_space = pl.BlockSpec(memory_space=pl.ANY)
    vmem = pl.BlockSpec(memory_space=pltpu.VMEM)
    token = jax.ShapeDtypeStruct((1, ROWS, WIDTH), BF16)
    outs = (token,) * 5 + (jax.ShapeDtypeStruct(lat.shape, BF16),)
    tokens = pltpu.VMEM((DOC, COLS), BF16)
    latents = pltpu.VMEM((GROUP, 2, LAT, COLS), BF16)
    dma = pltpu.SemaphoreType.DMA
    results = pl.pallas_call(
        functools.partial(kernel, x_count, z_count),
        name="attention",
        out_shape=outs + (jax.ShapeDtypeStruct((GROUP * HEADS, E), F32),),
        in_specs=[any_space] * 7 + [vmem],
        out_specs=[any_space] * 6 + [vmem],
        scratch_shapes=[
            tokens, tokens, tokens, tokens, tokens, latents, pltpu.VMEM((GROUP, 1, ROWS), jnp.int32),
            tokens, tokens, tokens, tokens, tokens, latents,
            pltpu.VMEM((DOC, COLS), F32), pltpu.VMEM((DOC, E), F32), pltpu.VMEM((DOC, E), F32),
            pltpu.VMEM((8, E), F32), pltpu.VMEM((x_count, 8, E), F32),
            pltpu.VMEM((z_count, 8, E), F32), pltpu.VMEM((GROUP, 8, E), F32),
            dma((7,)), dma((7,)), dma((6, HEADS)), dma((6, HEADS)),
            dma((x_count,)), dma((x_count,)), dma((z_count,)), dma((z_count,)), dma((GROUP,)), dma((GROUP,)),
        ],
        compiler_params=pltpu.CompilerParams(
            collective_id=0, has_side_effects=True, vmem_limit_bytes=48 << 20
        ),
    )(q, k, v, qc, lat, cot, media, gate.reshape(GROUP * HEADS, E))
    done = pl.pallas_call(
        finish_kernel,
        name="finish",
        out_shape=outs,
        in_specs=[any_space] * 6,
        out_specs=[any_space] * 6,
        scratch_shapes=[dma((6,))],
    )(*results[:6])
    return (*done, results[6].reshape(WIDTH))


def solution(mesh):
    token = P("doc", "seq", None)
    latent = P("doc", "seq", None, None, None)
    return jax.shard_map(
        functools.partial(per_device, mesh.shape["seq"] // GROUP, mesh.shape["doc"]),
        mesh=mesh,
        in_specs=(token, token, token, token, latent, P("doc", "seq"), P(), token),
        out_specs=(token, token, token, token, token, latent, P()),
        check_vma=False,
    )
```

```python
import functools

import jax
import jax.numpy as jnp
from jax import lax
from jax.experimental import pallas as pl
from jax.experimental.pallas import tpu as pltpu
from jax.sharding import PartitionSpec as P

E = 128
LAT = 64
GROUP = 8
ROWS = 128
DOC = GROUP * ROWS
HEADS = 4
COLS = HEADS * E
KEYS = GROUP * LAT
BLOCK = 256
WIDTH = GROUP * COLS
SCALE = E**-0.5
NEG_FILL = -1e30
MESH = pl.DeviceIdType.MESH
F32 = jnp.float32
BF16 = jnp.bfloat16


def dot(left, right, left_dim, right_dim):
    return lax.dot_general(
        left, right, (((left_dim,), (right_dim,)), ((), ())), preferred_element_type=F32
    )


def softmax_and_grad(scores, weights_grad_of, inverse_of):
    peak = jnp.max(scores, axis=0, keepdims=True)
    weights = jnp.exp(SCALE * (scores - peak))
    weights = weights * inverse_of(jnp.sum(weights, axis=0, keepdims=True))
    half = weights.astype(BF16)
    weights_grad = weights_grad_of()
    inner = jnp.sum(weights * weights_grad, axis=0, keepdims=True)
    return half, (weights * (weights_grad - inner)).astype(BF16)


def cross_head(head, gate_row, media_row, qc_buf, cot_buf, lat_buf, mixed, gqc_buf, glat_buf, acc_k, acc_v):
    cols = pl.ds(pl.multiple_of(head * E, E), E)
    keys = lat_buf[:, 0, :, cols].reshape(KEYS, E)
    values = lat_buf[:, 1, :, cols].reshape(KEYS, E)
    tanh_gate = jnp.tanh(gate_row)
    slot = lax.broadcasted_iota(jnp.int32, (KEYS, BLOCK), 0) // LAT
    acc_k[pl.ds(0, KEYS), :] = jnp.zeros((KEYS, E), F32)
    acc_v[pl.ds(0, KEYS), :] = jnp.zeros((KEYS, E), F32)

    def step(i, gate_sum):
        rows = pl.ds(pl.multiple_of(i * BLOCK, BLOCK), BLOCK)
        cited = media_row(i)
        queries = qc_buf[rows, cols]
        cot = cot_buf[rows, cols].astype(F32)
        cot_cross = (cot * tanh_gate).astype(BF16)
        scores = dot(keys, queries, 1, 1)
        scores = jnp.where(slot == cited, scores, NEG_FILL)
        half, scores_grad = softmax_and_grad(
            scores,
            lambda: dot(values, cot_cross, 1, 1),
            lambda total: jnp.where(cited >= 0, 1.0 / total, 0.0),
        )
        out = dot(values, half, 0, 0).T
        mixed[rows, cols] = tanh_gate * out
        acc_v[pl.ds(0, KEYS), :] += dot(half, cot_cross, 1, 0)
        gqc_buf[rows, cols] = (SCALE * dot(keys, scores_grad, 0, 0)).T.astype(BF16)
        acc_k[pl.ds(0, KEYS), :] += dot(scores_grad, queries, 1, 0)
        return gate_sum + jnp.sum(cot * out, axis=0, keepdims=True)

    gate_sum = lax.fori_loop(0, DOC // BLOCK, step, jnp.zeros((1, E), F32))
    glat_buf[:, 0, :, cols] = (SCALE * acc_k[pl.ds(0, KEYS), :]).astype(BF16).reshape(GROUP, LAT, E)
    glat_buf[:, 1, :, cols] = acc_v[pl.ds(0, KEYS), :].astype(BF16).reshape(GROUP, LAT, E)
    return gate_sum * (1.0 - tanh_gate * tanh_gate)


def self_head(head, q_buf, k_buf, v_buf, cot_buf, mixed, out_buf, gq_buf, gk_buf, gv_buf, acc_k, acc_v):
    cols = pl.ds(pl.multiple_of(head * E, E), E)
    acc_k[...] = jnp.zeros((DOC, E), F32)
    acc_v[...] = jnp.zeros((DOC, E), F32)
    for i in range(DOC // BLOCK):
        rows = pl.ds(i * BLOCK, BLOCK)
        seen = pl.ds(0, (i + 1) * BLOCK)
        queries = q_buf[rows, cols]
        cot = cot_buf[rows, cols]
        keys = k_buf[seen, cols]
        values = v_buf[seen, cols]
        scores = dot(keys, queries, 1, 1)
        shape = scores.shape
        causal = lax.broadcasted_iota(jnp.int32, shape, 0) <= i * BLOCK + lax.broadcasted_iota(jnp.int32, shape, 1)
        scores = jnp.where(causal, scores, -jnp.inf)
        half, scores_grad = softmax_and_grad(
            scores, lambda: dot(values, cot, 1, 1), lambda total: 1.0 / total
        )
        out = dot(values, half, 0, 0).T
        out_buf[rows, cols] = (out + mixed[rows, cols]).astype(BF16)
        acc_v[seen, :] += dot(half, cot, 1, 0)
        gq_buf[rows, cols] = (SCALE * dot(keys, scores_grad, 0, 0)).T.astype(BF16)
        acc_k[seen, :] += dot(scores_grad, queries, 1, 0)
    gk_buf[:, cols] = (SCALE * acc_k[...]).astype(BF16)
    gv_buf[:, cols] = acc_v[...].astype(BF16)


def kernel(
    x_count, z_count,
    q_ref, k_ref, v_ref, qc_ref, lat_ref, cot_ref, media_ref, gate_ref,
    out_ref, gq_ref, gk_ref, gv_ref, gqc_ref, glat_ref, gate_out_ref,
    q_buf, k_buf, v_buf, qc_buf, cot_buf, lat_buf, media_buf,
    out_buf, gq_buf, gk_buf, gv_buf, gqc_buf, glat_buf,
    mixed, acc_k, acc_v, gate_buf, gate_own, gate_all, gate_sums, gate_in,
    gate_sem, in_send, in_recv, out_send, out_recv, gather_recv, gate_send, gate_recv, spread_send,
):
    seq = lax.axis_index("seq")
    doc = lax.axis_index("doc")
    x = seq // GROUP
    me = lax.rem(seq, GROUP)

    def in_group(k):
        rank = lax.rem(me + k, GROUP)
        return rank, {"seq": x * GROUP + rank}

    leads = me == 0
    group_at = x + x_count * doc
    stages = (x_count * z_count).bit_length() - 1

    def partner(stage):
        bit = 1 << stage
        other = group_at + bit - 2 * bit * lax.rem(group_at // bit, 2)
        return {"seq": lax.rem(other, x_count) * GROUP, "doc": other // x_count}

    barrier = pltpu.get_barrier_semaphore()

    def greet(device):
        pl.semaphore_signal(barrier, inc=1, device_id=device, device_id_type=MESH)

    def greet_group(k, c):
        greet(in_group(k)[1])
        return c

    lax.fori_loop(1, GROUP, greet_group, 0)

    @pl.when(leads)
    def _():
        for stage in range(stages):
            greet(partner(stage))
        pl.semaphore_wait(barrier, GROUP - 1 + stages)

    @pl.when(jnp.logical_not(leads))
    def _():
        pl.semaphore_wait(barrier, GROUP - 1)

    own_rows = pl.ds(pl.multiple_of(me * ROWS, ROWS), ROWS)
    gate_load = pltpu.make_async_copy(gate_ref, gate_buf, gate_sem)
    gate_load.start()
    gate_own[...] = jnp.zeros_like(gate_own)

    def in_views(t, rank):
        cols = pl.ds(pl.multiple_of(rank * COLS, COLS), COLS)
        if t == 0:
            return media_ref, media_buf.at[me]
        if t == 1:
            return lat_ref.at[0, 0, :, :, cols], lat_buf.at[me]
        ref, buf = {2: (cot_ref, cot_buf), 3: (qc_ref, qc_buf), 4: (k_ref, k_buf), 5: (q_ref, q_buf), 6: (v_ref, v_buf)}[t]
        return ref.at[0, :, cols], buf.at[own_rows]

    for part in ((0, 1, 2, 3), (4, 5, 6)):
        for t in part:
            src, dst = in_views(t, me)
            pltpu.make_async_copy(src, dst, in_recv.at[t]).start()

        def send(k, c, part=part):
            rank, device = in_group(k)
            for t in part:
                src, dst = in_views(t, rank)
                pltpu.make_async_remote_copy(
                    src_ref=src, dst_ref=dst, send_sem=in_send.at[t], recv_sem=in_recv.at[t],
                    device_id=device, device_id_type=MESH,
                ).start()
            return c

        lax.fori_loop(1, GROUP, send, 0)

    def await_bytes(ref, sem):
        pltpu.make_async_copy(ref, ref, sem).wait()

    in_bufs = (media_buf, lat_buf, cot_buf, qc_buf, k_buf, q_buf, v_buf)

    def out_views(t, head, rank):
        there = pl.ds(pl.multiple_of(me * COLS + head * E, E), E)
        here = pl.ds(pl.multiple_of(head * E, E), E)
        if t == 5:
            return glat_buf.at[rank, :, :, here], glat_ref.at[0, 0, :, :, there]
        ref, buf = ((out_ref, out_buf), (gq_ref, gq_buf), (gk_ref, gk_buf), (gv_ref, gv_buf), (gqc_ref, gqc_buf))[t]
        return buf.at[pl.ds(pl.multiple_of(rank * ROWS, ROWS), ROWS), here], ref.at[0, :, there]

    def send_out(head, part):
        for t in part:
            src, dst = out_views(t, head, me)
            pltpu.make_async_copy(src, dst, out_recv.at[t, head]).start()

        def send(k, c):
            rank, device = in_group(k)
            for t in part:
                src, dst = out_views(t, head, rank)
                pltpu.make_async_remote_copy(
                    src_ref=src, dst_ref=dst, send_sem=out_send.at[t, head], recv_sem=out_recv.at[t, head],
                    device_id=device, device_id_type=MESH,
                ).start()
            return c

        lax.fori_loop(1, GROUP, send, 0)

    for t in (0, 1, 2, 3):
        await_bytes(in_bufs[t], in_recv.at[t])
    gate_load.wait()
    first_slot = x * GROUP

    def media_row(i):
        pair = jnp.concatenate([media_buf[2 * i], media_buf[2 * i + 1]], axis=1)
        return jnp.where(pair >= 0, pair - first_slot, -1)

    def cross_step(head, c):
        gate_row = gate_buf[pl.ds(me * HEADS + head, 1), :]
        gate_own[pl.ds(head, 1), :] = cross_head(
            head, gate_row, media_row, qc_buf, cot_buf, lat_buf, mixed, gqc_buf, glat_buf, acc_k, acc_v
        )
        send_out(head, (4, 5))
        return c

    lax.fori_loop(0, HEADS, cross_step, 0)

    gate_all[me] = gate_own[...]
    first = {"seq": x * GROUP}

    @pl.when(jnp.logical_not(leads))
    def _():
        pltpu.make_async_remote_copy(
            src_ref=gate_own, dst_ref=gate_all.at[me], send_sem=gate_send.at[stages], recv_sem=gather_recv.at[me],
            device_id=first, device_id_type=MESH,
        ).start()

    for t in (4, 5, 6):
        await_bytes(in_bufs[t], in_recv.at[t])

    def self_step(head, c):
        self_head(head, q_buf, k_buf, v_buf, cot_buf, mixed, out_buf, gq_buf, gk_buf, gv_buf, acc_k, acc_v)
        send_out(head, (0, 1, 2, 3))
        return c

    lax.fori_loop(0, HEADS, self_step, 0)

    @pl.when(leads)
    def _():
        def gathered(rank, c):
            await_bytes(gate_all.at[rank], gather_recv.at[rank])
            return c

        lax.fori_loop(1, GROUP, gathered, 0)
        gate_sums[0] = gate_all[...]
        for stage in range(stages):
            copy = pltpu.make_async_remote_copy(
                src_ref=gate_sums.at[stage], dst_ref=gate_in.at[stage],
                send_sem=gate_send.at[stage], recv_sem=gate_recv.at[stage],
                device_id=partner(stage), device_id_type=MESH,
            )
            copy.start()
            copy.wait()
            gate_sums[stage + 1] = gate_sums[stage] + gate_in[stage]

        def spread(k, c):
            pltpu.make_async_remote_copy(
                src_ref=gate_sums.at[stages], dst_ref=gate_sums.at[stages],
                send_sem=spread_send.at[k], recv_sem=gate_recv.at[stages],
                device_id={"seq": x * GROUP + k}, device_id_type=MESH,
            ).start()
            return c

        def spread_end(k, c):
            await_bytes(gate_sums.at[stages], spread_send.at[k])
            return c

        lax.fori_loop(1, GROUP, spread, 0)
        lax.fori_loop(1, GROUP, spread_end, 0)

    @pl.when(jnp.logical_not(leads))
    def _():
        await_bytes(gate_own, gate_send.at[stages])
        await_bytes(gate_sums.at[stages], gate_recv.at[stages])

    for rank in range(GROUP):
        gate_out_ref[pl.ds(rank * HEADS, HEADS), :] = gate_sums[stages, rank, pl.ds(0, HEADS), :]

    most = GROUP - 1
    for t, buf in enumerate(in_bufs):
        await_bytes(buf.at[pl.ds(0, most * (buf.shape[0] // GROUP))], in_send.at[t])

    def end(head, c):
        here = pl.ds(pl.multiple_of(head * E, E), E)
        for t, buf in enumerate((out_buf, gq_buf, gk_buf, gv_buf, gqc_buf)):
            await_bytes(buf.at[pl.ds(0, most * ROWS), here], out_send.at[t, head])
            await_bytes(buf.at[:, here], out_recv.at[t, head])
        await_bytes(glat_buf.at[pl.ds(0, most), :, :, here], out_send.at[5, head])
        await_bytes(glat_buf.at[:, :, :, here], out_recv.at[5, head])
        return c

    lax.fori_loop(0, HEADS, end, 0)


def finish_kernel(*refs):
    count = len(refs) // 2
    sems = refs[-1]
    copies = [pltpu.make_async_copy(refs[i], refs[count + i], sems.at[i]) for i in range(count)]
    for copy in copies:
        copy.start()
    for copy in copies:
        copy.wait()


def per_device(x_count, z_count, q, k, v, qc, lat, media, gate, cot):
    hbm = pl.BlockSpec(memory_space=pl.ANY)
    vmem = pl.BlockSpec(memory_space=pltpu.VMEM)
    token = jax.ShapeDtypeStruct((1, ROWS, WIDTH), BF16)
    gate_shape = (GROUP * HEADS, E)
    stages = (x_count * z_count).bit_length() - 1
    outs = (token,) * 5 + (jax.ShapeDtypeStruct(lat.shape, BF16), jax.ShapeDtypeStruct(gate_shape, F32))
    tokens = pltpu.VMEM((DOC, COLS), BF16)
    latents = pltpu.VMEM((GROUP, 2, LAT, COLS), BF16)
    dma = pltpu.SemaphoreType.DMA
    results = pl.pallas_call(
        functools.partial(kernel, x_count, z_count),
        name="attention",
        out_shape=outs,
        in_specs=[hbm] * 8,
        out_specs=[hbm] * 6 + [vmem],
        scratch_shapes=[
            tokens, tokens, tokens, tokens, tokens, latents, pltpu.VMEM((GROUP, 1, ROWS), jnp.int32),
            tokens, tokens, tokens, tokens, tokens, latents,
            pltpu.VMEM((DOC, COLS), F32), pltpu.VMEM((DOC, E), F32), pltpu.VMEM((DOC, E), F32),
            pltpu.VMEM(gate_shape, F32), pltpu.VMEM((8, E), F32), pltpu.VMEM((GROUP, 8, E), F32),
            pltpu.VMEM((stages + 1, GROUP, 8, E), F32), pltpu.VMEM((stages, GROUP, 8, E), F32),
            dma(()), dma((7,)), dma((7,)), dma((6, HEADS)), dma((6, HEADS)),
            dma((GROUP,)), dma((stages + 1,)), dma((stages + 1,)), dma((GROUP,)),
        ],
        compiler_params=pltpu.CompilerParams(
            collective_id=0, has_side_effects=True, vmem_limit_bytes=47 << 20
        ),
    )(q, k, v, qc, lat, cot, media, gate.reshape(gate_shape))
    done = pl.pallas_call(
        finish_kernel,
        name="finish",
        out_shape=outs,
        in_specs=[vmem] * 7,
        out_specs=[hbm] * 7,
        scratch_shapes=[dma((7,))],
        compiler_params=pltpu.CompilerParams(vmem_limit_bytes=47 << 20),
    )(*results)
    return (*done[:6], done[6].reshape(WIDTH))


def solution(mesh):
    token = P("doc", "seq", None)
    latent = P("doc", "seq", None, None, None)
    return jax.shard_map(
        functools.partial(per_device, mesh.shape["seq"] // GROUP, mesh.shape["doc"]),
        mesh=mesh,
        in_specs=(token, token, token, token, latent, P("doc", "seq"), P(), token),
        out_specs=(token, token, token, token, token, latent, P()),
        check_vma=False,
    )
```

```python
import functools

import jax
import jax.numpy as jnp
from jax import lax
from jax.experimental import pallas as pl
from jax.experimental.pallas import tpu as pltpu
from jax.sharding import PartitionSpec as P

E = 128
LAT = 64
GROUP = 8
ROWS = 128
BLOCK = 256
DOC = GROUP * ROWS
KEYS = GROUP * LAT
A, B = 0, 1
HEADS = (5, 3)
BATCHES = (((0, 2), (2, 3)), ((0, 3),))
HERE = (0, 5)
THERE = (0, 20)
ALL_HEADS = 32
WIDTH = ALL_HEADS * E
COLS = sum(HEADS) * E
SCALE = E**-0.5
NEG_FILL = -1e30
MESH = pl.DeviceIdType.MESH
F32 = jnp.float32
BF16 = jnp.bfloat16


def dot(left, right, left_dim, right_dim):
    return lax.dot_general(
        left, right, (((left_dim,), (right_dim,)), ((), ())), preferred_element_type=F32
    )


def softmax_and_grad(scores, weights_grad_of, inverse_of):
    peak = jnp.max(scores, axis=0, keepdims=True)
    weights = jnp.exp(SCALE * (scores - peak))
    weights = weights * inverse_of(jnp.sum(weights, axis=0, keepdims=True))
    half = weights.astype(BF16)
    weights_grad = weights_grad_of()
    inner = jnp.sum(weights * weights_grad, axis=0, keepdims=True)
    return half, (weights * (weights_grad - inner)).astype(BF16)


def head_cols(job, head):
    return pl.ds(pl.multiple_of((HERE[job] + head) * E, E), E)


def cross_head(cols, gate_row, media_row, qc_buf, cot_buf, lat_buf, mixed, gqc_buf, glat_buf):
    keys = lat_buf[:, 0, :, cols].reshape(KEYS, E)
    values = lat_buf[:, 1, :, cols].reshape(KEYS, E)
    tanh_gate = jnp.tanh(gate_row)
    slot = lax.broadcasted_iota(jnp.int32, (KEYS, BLOCK), 0) // LAT
    gate_sum = jnp.zeros((1, E), F32)
    keys_grad = jnp.zeros((KEYS, E), F32)
    values_grad = jnp.zeros((KEYS, E), F32)
    for i in range(2):
        rows = pl.ds(i * BLOCK, BLOCK)
        cited = media_row(i)
        queries = qc_buf[rows, cols]
        cot = cot_buf[rows, cols].astype(F32)
        cot_cross = (cot * tanh_gate).astype(BF16)
        scores = dot(keys, queries, 1, 1)
        scores = jnp.where(slot == cited, scores, NEG_FILL)
        half, scores_grad = softmax_and_grad(
            scores,
            lambda: dot(values, cot_cross, 1, 1),
            lambda total: jnp.where(cited >= 0, 1.0 / total, 0.0),
        )
        out = dot(values, half, 0, 0).T
        mixed[rows, cols] = tanh_gate * out
        values_grad += dot(half, cot_cross, 1, 0)
        gqc_buf[rows, cols] = (SCALE * dot(keys, scores_grad, 0, 0)).T.astype(BF16)
        keys_grad += dot(scores_grad, queries, 1, 0)
        gate_sum += jnp.sum(cot * out, axis=0, keepdims=True)
    glat_buf[:, 0, :, cols] = (SCALE * keys_grad).astype(BF16).reshape(GROUP, LAT, E)
    glat_buf[:, 1, :, cols] = values_grad.astype(BF16).reshape(GROUP, LAT, E)
    return gate_sum * (1.0 - tanh_gate * tanh_gate)


def self_block(i, place, cols, q_buf, k_buf, v_buf, cot_buf, mixed, out_buf, gq_buf, acc_k, acc_v):
    rows = pl.ds(place * BLOCK, BLOCK)
    seen = pl.ds(0, (i + 1) * BLOCK)
    queries = q_buf[rows, cols]
    cot = cot_buf[rows, cols]
    keys = k_buf[seen, cols]
    values = v_buf[seen, cols]
    scores = dot(keys, queries, 1, 1)
    shape = scores.shape
    causal = lax.broadcasted_iota(jnp.int32, shape, 0) <= i * BLOCK + lax.broadcasted_iota(jnp.int32, shape, 1)
    scores = jnp.where(causal, scores, -jnp.inf)
    half, scores_grad = softmax_and_grad(
        scores, lambda: dot(values, cot, 1, 1), lambda total: 1.0 / total
    )
    out = dot(values, half, 0, 0).T
    out_buf[rows, cols] = (out + mixed[rows, cols]).astype(BF16)
    acc_v[seen, :] += dot(half, cot, 1, 0)
    gq_buf[rows, cols] = (SCALE * dot(keys, scores_grad, 0, 0)).T.astype(BF16)
    acc_k[seen, :] += dot(scores_grad, queries, 1, 0)


def kernel(
    x_count, z_count,
    q_ref, k_ref, v_ref, qc_ref, lat_ref, cot_ref, media_ref, gate_ref,
    out_ref, gq_ref, gk_ref, gv_ref, gqc_ref, glat_ref, gate_out_ref,
    q_buf, qc_buf, cot_buf, k_buf, v_buf, lat_buf, media_buf,
    out_buf, gq_buf, gqc_buf, gk_buf, gv_buf, glat_buf, gk_in, gv_in, glat_in,
    mixed, acc_k, acc_v, gate_buf, gate_own, gate_all, gate_sums, gate_in,
    gate_sem, media_send, media_recv, in_send, in_recv, pass_send, pass_recv, part_send, part_recv,
    out_send, out_recv, gather_recv, gate_send, gate_recv, spread_send,
):
    seq = lax.axis_index("seq")
    doc = lax.axis_index("doc")
    x = seq // GROUP
    me = lax.rem(seq, GROUP)
    chip = me // 2
    core = lax.rem(me, 2)
    mirror = 3 - chip
    pair = chip + 1 - 2 * lax.rem(chip, 2)
    homes = ((chip, mirror), (chip, pair))
    partner = (pair, mirror)
    inner = lax.rem((chip + 1) // 2, 2)
    low = chip < 2
    is_inner = inner == 1
    not_ = jnp.logical_not

    def at(chip, core):
        return {"seq": x * GROUP + chip * 2 + core}

    def in_group(k):
        rank = lax.rem(me + k, GROUP)
        return rank, {"seq": x * GROUP + rank}

    leads = me == 0
    group_at = x + x_count * doc
    stages = (x_count * z_count).bit_length() - 1

    def gate_partner(stage):
        bit = 1 << stage
        other = group_at + bit - 2 * bit * lax.rem(group_at // bit, 2)
        return {"seq": lax.rem(other, x_count) * GROUP, "doc": other // x_count}

    barrier = pltpu.get_barrier_semaphore()

    def greet(device):
        pl.semaphore_signal(barrier, inc=1, device_id=device, device_id_type=MESH)

    def greet_group(k, c):
        greet(in_group(k)[1])
        return c

    lax.fori_loop(1, GROUP, greet_group, 0)

    @pl.when(leads)
    def _():
        for stage in range(stages):
            greet(gate_partner(stage))
        pl.semaphore_wait(barrier, GROUP - 1 + stages)

    @pl.when(not_(leads))
    def _():
        pl.semaphore_wait(barrier, GROUP - 1)

    def send(src, dst, send_sem, recv_sem, device):
        pltpu.make_async_remote_copy(
            src_ref=src, dst_ref=dst, send_sem=send_sem, recv_sem=recv_sem,
            device_id=device, device_id_type=MESH,
        ).start()

    def await_bytes(ref, sem):
        pltpu.make_async_copy(ref, ref, sem).wait()

    def here(job):
        return pl.ds(HERE[job] * E, HEADS[job] * E)

    def first_head(job, chip, core):
        plan = chip // 2 if job == A else lax.rem((chip + 1) // 2, 2)
        return THERE[job] + (plan * 2 + core) * HEADS[job]

    def there(job, chip, core):
        return pl.ds(pl.multiple_of(first_head(job, chip, core) * E, E), HEADS[job] * E)

    def place(job, chip):
        return chip // 2 if job == A else lax.rem(chip, 2)

    def rows_at(block, core):
        return pl.ds(pl.multiple_of(block * BLOCK + core * ROWS, ROWS), ROWS)

    gate_load = pltpu.make_async_copy(gate_ref, gate_buf, gate_sem)
    gate_load.start()
    pltpu.make_async_copy(media_ref, media_buf.at[me], media_recv).start()

    def send_media(k, c):
        send(media_ref, media_buf.at[me], media_send, media_recv, in_group(k)[1])
        return c

    lax.fori_loop(1, GROUP, send_media, 0)

    K, V, LATS, COT, QC, Q = range(6)
    refs = (k_ref, v_ref, lat_ref, cot_ref, qc_ref, q_ref)
    bufs = (k_buf, v_buf, lat_buf, cot_buf, qc_buf, q_buf)

    def in_views(t, job, to_chip, to_core):
        cols = there(job, to_chip, to_core)
        if t == LATS:
            return lat_ref.at[0, 0, :, :, cols], lat_buf.at[me, :, :, here(job)]
        rows = rows_at(chip, core) if t in (K, V) else rows_at(place(job, chip), core)
        return refs[t].at[0, :, cols], bufs[t].at[rows, here(job)]

    def send_in(t, job):
        src, dst = in_views(t, job, chip, core)
        pltpu.make_async_copy(src, dst, in_recv.at[job, t]).start()
        for to_chip, to_core in ((homes[job][1], core), (homes[job][1], 1 - core), (chip, 1 - core)):
            src, dst = in_views(t, job, to_chip, to_core)
            send(src, dst, in_send.at[job, t], in_recv.at[job, t], at(to_chip, to_core))

    for t in (LATS, K, V, COT, QC, Q):
        send_in(t, A)
        if t != Q:
            send_in(t, B)

    def await_in(t, job):
        if t == LATS:
            await_bytes(lat_buf.at[pl.ds(0, 4), :, :, here(job)], in_recv.at[job, t])
        else:
            await_bytes(q_buf.at[:, here(job)], in_recv.at[job, t])

    def pass_on(job, t, first, count):
        part = bufs[t].at[pl.ds(first, count), :, :, here(job)] if t == LATS else bufs[t].at[pl.ds(first, count), here(job)]
        send(part, part, pass_send.at[job, t], pass_recv.at[job, t], at(partner[job], core))

    for job in (A, B):
        await_in(LATS, job)
    pl.when(not_(is_inner))(lambda: (pass_on(A, LATS, 0, 2), pass_on(A, LATS, 6, 2)) and None)
    pl.when(is_inner)(lambda: pass_on(A, LATS, 2, 4))
    pl.when(low)(lambda: pass_on(B, LATS, 0, 4))
    pl.when(not_(low))(lambda: pass_on(B, LATS, 4, 4))
    for t in (K, V):
        for job in (A, B):
            await_in(t, job)
        pl.when(not_(is_inner))(lambda: pass_on(A, t, 0, BLOCK))
        pl.when(is_inner)(lambda: pass_on(A, t, BLOCK, 2 * BLOCK))
        pl.when(low)(lambda: pass_on(B, t, 0, 2 * BLOCK))
    send_in(Q, B)

    OUT, GQ, GQC, GK, GV, GLAT = range(6)
    out_refs = (out_ref, gq_ref, gqc_ref, gk_ref, gv_ref, glat_ref)
    out_bufs = (out_buf, gq_buf, gqc_buf, gk_buf, gv_buf, glat_buf)

    def out_views(t, job, to_chip, to_core, first, count):
        near = pl.ds((HERE[job] + first) * E, count * E)
        far = pl.ds(pl.multiple_of((first_head(job, chip, core) + first) * E, E), count * E)
        if t == GLAT:
            return glat_buf.at[to_chip * 2 + to_core, :, :, near], glat_ref.at[0, 0, :, :, far]
        rows = rows_at(to_chip, to_core) if t in (GK, GV) else rows_at(place(job, to_chip), to_core)
        return out_bufs[t].at[rows, near], out_refs[t].at[0, :, far]

    def send_home(job, part, first=0, count=None):
        count = count or HEADS[job]
        for t in part:
            src, dst = out_views(t, job, chip, core, first, count)
            pltpu.make_async_copy(src, dst, out_recv.at[t]).start()
            for to_chip, to_core in ((homes[job][1], core), (homes[job][1], 1 - core), (chip, 1 - core)):
                src, dst = out_views(t, job, to_chip, to_core, first, count)
                send(src, dst, out_send.at[job, t], out_recv.at[t], at(to_chip, to_core))

    await_bytes(media_buf, media_recv)
    gate_load.wait()
    first_slot = x * GROUP

    def send_glat(job, first, count):
        send(
            glat_buf.at[pl.ds(first, count), :, :, here(job)], glat_in.at[pl.ds(first, count), :, :, here(job)],
            part_send.at[job, 2], part_recv.at[job, 2], at(partner[job], core),
        )

    for job in (A, B):
        await_in(COT, job)
        await_in(QC, job)
        await_bytes(lat_buf.at[pl.ds(0, 4), :, :, here(job)], pass_recv.at[job, LATS])
        head_of = first_head(job, chip, core)

        def media_row(i, job=job):
            block = (3 * i * (1 - inner) + (1 + i) * inner) if job == A else 2 * (chip // 2) + i
            cited = jnp.concatenate([media_buf[2 * block], media_buf[2 * block + 1]], axis=1)
            return jnp.where(cited >= 0, cited - first_slot, -1)

        def cross_step(head, c, job=job, head_of=head_of, media_row=media_row):
            gate_own[pl.ds(HERE[job] + head, 1), :] = cross_head(
                head_cols(job, head), gate_buf[pl.ds(head_of + head, 1), :], media_row,
                qc_buf, cot_buf, lat_buf, mixed, gqc_buf, glat_buf,
            )
            return c

        lax.fori_loop(0, HEADS[job], cross_step, 0)
        if job == B:
            gate_all[me] = gate_own[...]

            @pl.when(not_(leads))
            def _():
                send(gate_own, gate_all.at[me], gate_send.at[stages], gather_recv.at[me], {"seq": x * GROUP})

        if job == A:
            pl.when(not_(is_inner))(lambda: send_glat(A, 2, 4))
            pl.when(is_inner)(lambda: (send_glat(A, 0, 2), send_glat(A, 6, 2)) and None)
        else:
            pl.when(low)(lambda: send_glat(B, 4, 4))
            pl.when(not_(low))(lambda: send_glat(B, 0, 4))
        send_home(job, (GQC,))

    def send_part(job, first_row, row_count, first, count):
        rows, cols = pl.ds(first_row, row_count), pl.ds((HERE[job] + first) * E, count * E)
        for t, (buf, into) in enumerate(((gk_buf, gk_in), (gv_buf, gv_in))):
            send(buf.at[rows, cols], into.at[rows, cols], part_send.at[job, t], part_recv.at[job, t], at(partner[job], core))

    for job in (A, B):
        await_in(Q, job)
        for t in (K, V):
            if job == A:
                pl.when(not_(is_inner))(lambda: await_bytes(k_buf.at[pl.ds(0, 2 * BLOCK), here(A)], pass_recv.at[A, t]))
                pl.when(is_inner)(lambda: await_bytes(k_buf.at[pl.ds(0, BLOCK), here(A)], pass_recv.at[A, t]))
            else:
                pl.when(not_(low))(lambda: await_bytes(k_buf.at[pl.ds(0, 2 * BLOCK), here(B)], pass_recv.at[B, t]))

        def self_step(head, c, job=job):
            cols = head_cols(job, head)
            acc_k[...] = jnp.zeros((DOC, E), F32)
            acc_v[...] = jnp.zeros((DOC, E), F32)

            def block(i):
                self_block(
                    i, place(job, i) if job == A else i % 2, cols,
                    q_buf, k_buf, v_buf, cot_buf, mixed, out_buf, gq_buf, acc_k, acc_v,
                )

            if job == A:
                pl.when(not_(is_inner))(lambda: (block(0), block(3)) and None)
                pl.when(is_inner)(lambda: (block(1), block(2)) and None)
            else:
                pl.when(low)(lambda: (block(0), block(1)) and None)
                pl.when(not_(low))(lambda: (block(2), block(3)) and None)
            gk_buf[:, cols] = (SCALE * acc_k[...]).astype(BF16)
            gv_buf[:, cols] = acc_v[...].astype(BF16)
            for first, count in BATCHES[job]:

                @pl.when(head == first + count - 1)
                def _(first=first, count=count):
                    if job == A:
                        pl.when(not_(is_inner))(lambda: send_part(A, BLOCK, 2 * BLOCK, first, count))
                        pl.when(is_inner)(lambda: send_part(A, 0, BLOCK, first, count))
                    else:
                        pl.when(not_(low))(lambda: send_part(B, 0, 2 * BLOCK, first, count))
                    send_home(job, (OUT, GQ), first, count)

            return c

        lax.fori_loop(0, HEADS[job], self_step, 0)

    def add(buf, into, *where):
        buf[where] = (buf[where].astype(F32) + into[where].astype(F32)).astype(BF16)

    def add_glat(job, first, count):
        add(glat_buf, glat_in, pl.ds(first, count), slice(None), slice(None), here(job))

    def add_part(job, t, first, count):
        buf, into = ((gk_buf, gk_in), (gv_buf, gv_in))[t]
        await_bytes(into.at[pl.ds(first, count), here(job)], part_recv.at[job, t])
        add(buf, into, pl.ds(first, count), here(job))

    def finish_glat(job):
        await_bytes(glat_in.at[pl.ds(0, 4), :, :, here(job)], part_recv.at[job, 2])
        if job == A:
            pl.when(not_(is_inner))(lambda: (add_glat(A, 0, 2), add_glat(A, 6, 2)) and None)
            pl.when(is_inner)(lambda: add_glat(A, 2, 4))
        else:
            pl.when(low)(lambda: add_glat(B, 0, 4))
            pl.when(not_(low))(lambda: add_glat(B, 4, 4))
        send_home(job, (GLAT,))

    def finish_part(job):
        for t, result in enumerate((GK, GV)):
            if job == A:
                pl.when(not_(is_inner))(lambda: add_part(A, t, 0, BLOCK))
                pl.when(is_inner)(lambda: add_part(A, t, BLOCK, 2 * BLOCK))
            else:
                pl.when(low)(lambda: add_part(B, t, 0, 2 * BLOCK))
            send_home(job, (result,))

    def gate_copy(stage):
        return pltpu.make_async_remote_copy(
            src_ref=gate_sums.at[stage], dst_ref=gate_in.at[stage],
            send_sem=gate_send.at[stage], recv_sem=gate_recv.at[stage],
            device_id=gate_partner(stage), device_id_type=MESH,
        )

    def gate_stage(stage):
        @pl.when(leads)
        def _():
            if stage == 0:
                def gathered(rank, c):
                    await_bytes(gate_all.at[rank], gather_recv.at[rank])
                    return c

                lax.fori_loop(1, GROUP, gathered, 0)
                gate_sums[0] = gate_all[...]
            else:
                gate_copy(stage - 1).wait()
                gate_sums[stage] = gate_sums[stage - 1] + gate_in[stage - 1]
            if stage < stages:
                gate_copy(stage).start()
            else:
                def spread(k, c):
                    send(
                        gate_sums.at[stages], gate_sums.at[stages], spread_send.at[k], gate_recv.at[stages],
                        {"seq": x * GROUP + k},
                    )
                    return c

                lax.fori_loop(1, GROUP, spread, 0)

    gate_stage(0)
    finish_glat(A)
    gate_stage(1)
    finish_glat(B)
    gate_stage(2)
    finish_part(B)
    for stage in range(3, stages):
        gate_stage(stage)
    finish_part(A)
    gate_stage(stages)

    @pl.when(leads)
    def _():
        def spread_end(k, c):
            await_bytes(gate_sums.at[stages], spread_send.at[k])
            return c

        lax.fori_loop(1, GROUP, spread_end, 0)

    @pl.when(not_(leads))
    def _():
        await_bytes(gate_own, gate_send.at[stages])
        await_bytes(gate_sums.at[stages], gate_recv.at[stages])

    for job, owners in ((A, ((0, 1), (2, 3))), (B, ((0, 3), (1, 2)))):
        part = pl.ds(HERE[job], HEADS[job])
        for plan, (one, two) in enumerate(owners):
            for side in range(2):
                first = THERE[job] + (plan * 2 + side) * HEADS[job]
                gate_out_ref[pl.ds(first, HEADS[job]), :] = (
                    gate_sums[stages, one * 2 + side, part, :] + gate_sums[stages, two * 2 + side, part, :]
                )

    await_bytes(media_buf.at[pl.ds(0, GROUP - 1)], media_send)
    for job in (A, B):
        for t in range(6):
            sent = lat_buf.at[pl.ds(0, 3), :, :, here(job)] if t == LATS else q_buf.at[pl.ds(0, 3 * ROWS), here(job)]
            await_bytes(sent, in_send.at[job, t])
            sent = glat_buf.at[pl.ds(0, 3), :, :, here(job)] if t == GLAT else out_buf.at[pl.ds(0, 3 * ROWS), here(job)]
            await_bytes(sent, out_send.at[job, t])
        await_bytes(lat_buf.at[pl.ds(0, 4), :, :, here(job)], pass_send.at[job, LATS])
        await_bytes(glat_buf.at[pl.ds(0, 4), :, :, here(job)], part_send.at[job, 2])

    def sent_rows(job, rows, pass_only, part_only):
        for t in (0, 1):
            if pass_only:
                await_bytes(k_buf.at[pl.ds(0, rows), here(job)], pass_send.at[job, t])
            if part_only:
                await_bytes(gk_buf.at[pl.ds(0, rows), here(job)], part_send.at[job, t])

    @pl.when(is_inner)
    def _():
        sent_rows(A, 2 * BLOCK, True, False)
        sent_rows(A, BLOCK, False, True)

    @pl.when(not_(is_inner))
    def _():
        sent_rows(A, BLOCK, True, False)
        sent_rows(A, 2 * BLOCK, False, True)

    pl.when(low)(lambda: sent_rows(B, 2 * BLOCK, True, False))
    pl.when(not_(low))(lambda: sent_rows(B, 2 * BLOCK, False, True))
    for t in range(6):
        await_bytes(out_refs[t], out_recv.at[t])


def finish_kernel(*refs):
    count = len(refs) // 2
    sems = refs[-1]
    copies = [pltpu.make_async_copy(refs[i], refs[count + i], sems.at[i]) for i in range(count)]
    for copy in copies:
        copy.start()
    for copy in copies:
        copy.wait()


def per_device(x_count, z_count, q, k, v, qc, lat, media, gate, cot):
    anywhere = pl.BlockSpec(memory_space=pl.ANY)
    vmem = pl.BlockSpec(memory_space=pltpu.VMEM)
    token = jax.ShapeDtypeStruct((1, ROWS, WIDTH), BF16)
    gate_shape = (ALL_HEADS, E)
    stages = (x_count * z_count).bit_length() - 1
    outs = (token,) * 5 + (jax.ShapeDtypeStruct(lat.shape, BF16), jax.ShapeDtypeStruct(gate_shape, F32))
    queries = pltpu.VMEM((2 * BLOCK, COLS), BF16)
    tokens = pltpu.VMEM((DOC, COLS), BF16)
    latents = pltpu.VMEM((GROUP, 2, LAT, COLS), BF16)
    dma = pltpu.SemaphoreType.DMA
    results = pl.pallas_call(
        functools.partial(kernel, x_count, z_count),
        name="attention",
        out_shape=outs,
        in_specs=[anywhere] * 8,
        out_specs=[anywhere] * 6 + [vmem],
        scratch_shapes=[
            queries, queries, queries, tokens, tokens, latents, pltpu.VMEM((GROUP, 1, ROWS), jnp.int32),
            queries, queries, queries, tokens, tokens, latents, tokens, tokens, latents,
            pltpu.VMEM((2 * BLOCK, COLS), F32), pltpu.VMEM((DOC, E), F32), pltpu.VMEM((DOC, E), F32),
            pltpu.VMEM(gate_shape, F32), pltpu.VMEM((8, E), F32), pltpu.VMEM((GROUP, 8, E), F32),
            pltpu.VMEM((stages + 1, GROUP, 8, E), F32), pltpu.VMEM((stages, GROUP, 8, E), F32),
            dma(()), dma(()), dma(()), dma((2, 6)), dma((2, 6)), dma((2, 3)), dma((2, 3)), dma((2, 3)), dma((2, 3)),
            dma((2, 6)), dma((6,)), dma((GROUP,)), dma((stages + 1,)), dma((stages + 1,)), dma((GROUP,)),
        ],
        compiler_params=pltpu.CompilerParams(
            collective_id=0, has_side_effects=True, vmem_limit_bytes=95 << 19
        ),
    )(q, k, v, qc, lat, cot, media, gate.reshape(gate_shape))
    done = pl.pallas_call(
        finish_kernel,
        name="finish",
        out_shape=outs,
        in_specs=[vmem] * 7,
        out_specs=[anywhere] * 7,
        scratch_shapes=[dma((7,))],
        compiler_params=pltpu.CompilerParams(vmem_limit_bytes=47 << 20),
    )(*results)
    return (*done[:6], done[6].reshape(WIDTH))


def solution(mesh):
    token = P("doc", "seq", None)
    latent = P("doc", "seq", None, None, None)
    return jax.shard_map(
        functools.partial(per_device, mesh.shape["seq"] // GROUP, mesh.shape["doc"]),
        mesh=mesh,
        in_specs=(token, token, token, token, latent, P("doc", "seq"), P(), token),
        out_specs=(token, token, token, token, token, latent, P()),
        check_vma=False,
    )
```

```python
import functools

import jax
import jax.numpy as jnp
from jax import lax
from jax.experimental import pallas as pl
from jax.experimental.pallas import tpu as pltpu
from jax.sharding import PartitionSpec as P

E = 128
LAT = 64
GROUP = 8
ROWS = 128
BLOCK = 256
DOC = GROUP * ROWS
KEYS = GROUP * LAT
A, B = 0, 1
HEADS = (5, 3)
BATCHES = (((0, 1), (1, 2), (3, 2)), ((0, 3),))
HERE = (0, 5)
THERE = (0, 20)
ALL_HEADS = 32
WIDTH = ALL_HEADS * E
COLS = sum(HEADS) * E
SCALE = E**-0.5
NEG_FILL = -1e30
MESH = pl.DeviceIdType.MESH
F32 = jnp.float32
BF16 = jnp.bfloat16


def dot(left, right, left_dim, right_dim):
    return lax.dot_general(
        left, right, (((left_dim,), (right_dim,)), ((), ())), preferred_element_type=F32
    )


def softmax_and_grad(scores, weights_grad_of, inverse_of):
    peak = jnp.max(scores, axis=0, keepdims=True)
    weights = jnp.exp(SCALE * (scores - peak))
    weights = weights * inverse_of(jnp.sum(weights, axis=0, keepdims=True))
    half = weights.astype(BF16)
    weights_grad = weights_grad_of()
    inner = jnp.sum(weights * weights_grad, axis=0, keepdims=True)
    return half, (weights * (weights_grad - inner)).astype(BF16)


def head_cols(job, head):
    return pl.ds(pl.multiple_of((HERE[job] + head) * E, E), E)


def cross_head(cols, gate_row, media_row, qc_buf, cot_buf, lat_buf, mixed, gqc_buf, glat_buf):
    keys = lat_buf[:, 0, :, cols].reshape(KEYS, E)
    values = lat_buf[:, 1, :, cols].reshape(KEYS, E)
    tanh_gate = jnp.tanh(gate_row)
    slot = lax.broadcasted_iota(jnp.int32, (KEYS, BLOCK), 0) // LAT
    gate_sum = jnp.zeros((1, E), F32)
    keys_grad = jnp.zeros((KEYS, E), F32)
    values_grad = jnp.zeros((KEYS, E), F32)
    for i in range(2):
        rows = pl.ds(i * BLOCK, BLOCK)
        cited = media_row(i)
        queries = qc_buf[rows, cols]
        cot = cot_buf[rows, cols].astype(F32)
        cot_cross = (cot * tanh_gate).astype(BF16)
        scores = dot(keys, queries, 1, 1)
        scores = jnp.where(slot == cited, scores, NEG_FILL)
        half, scores_grad = softmax_and_grad(
            scores,
            lambda: dot(values, cot_cross, 1, 1),
            lambda total: jnp.where(cited >= 0, 1.0 / total, 0.0),
        )
        out = dot(values, half, 0, 0).T
        mixed[rows, cols] = tanh_gate * out
        values_grad += dot(half, cot_cross, 1, 0)
        gqc_buf[rows, cols] = (SCALE * dot(keys, scores_grad, 0, 0)).T.astype(BF16)
        keys_grad += dot(scores_grad, queries, 1, 0)
        gate_sum += jnp.sum(cot * out, axis=0, keepdims=True)
    glat_buf[:, 0, :, cols] = (SCALE * keys_grad).astype(BF16).reshape(GROUP, LAT, E)
    glat_buf[:, 1, :, cols] = values_grad.astype(BF16).reshape(GROUP, LAT, E)
    return gate_sum * (1.0 - tanh_gate * tanh_gate)


def self_block(i, place, cols, q_buf, k_buf, v_buf, cot_buf, mixed, out_buf, gq_buf, acc_k, acc_v):
    rows = pl.ds(place * BLOCK, BLOCK)
    seen = pl.ds(0, (i + 1) * BLOCK)
    queries = q_buf[rows, cols]
    cot = cot_buf[rows, cols]
    keys = k_buf[seen, cols]
    values = v_buf[seen, cols]
    scores = dot(keys, queries, 1, 1)
    shape = scores.shape
    causal = lax.broadcasted_iota(jnp.int32, shape, 0) <= i * BLOCK + lax.broadcasted_iota(jnp.int32, shape, 1)
    scores = jnp.where(causal, scores, -jnp.inf)
    half, scores_grad = softmax_and_grad(
        scores, lambda: dot(values, cot, 1, 1), lambda total: 1.0 / total
    )
    out = dot(values, half, 0, 0).T
    out_buf[rows, cols] = (out + mixed[rows, cols]).astype(BF16)
    acc_v[seen, :] += dot(half, cot, 1, 0)
    gq_buf[rows, cols] = (SCALE * dot(keys, scores_grad, 0, 0)).T.astype(BF16)
    acc_k[seen, :] += dot(scores_grad, queries, 1, 0)


def kernel(
    x_count, z_count,
    q_ref, k_ref, v_ref, qc_ref, lat_ref, cot_ref, media_ref, gate_ref,
    out_ref, gq_ref, gk_ref, gv_ref, gqc_ref, glat_ref, gate_out_ref,
    q_buf, qc_buf, cot_buf, k_buf, v_buf, lat_buf, media_buf,
    out_buf, gq_buf, gqc_buf, gk_buf, gv_buf, glat_buf, gk_in, gv_in, glat_in,
    mixed, acc_k, acc_v, gate_buf, gate_own, gate_all, gate_sums, gate_in,
    gate_sem, media_send, media_recv, in_send, in_recv, pass_send, pass_recv, part_send, part_recv,
    out_send, out_recv, gather_recv, gate_send, gate_recv, spread_send,
):
    seq = lax.axis_index("seq")
    doc = lax.axis_index("doc")
    x = seq // GROUP
    me = lax.rem(seq, GROUP)
    chip = me // 2
    core = lax.rem(me, 2)
    mirror = 3 - chip
    pair = chip + 1 - 2 * lax.rem(chip, 2)
    homes = ((chip, mirror), (chip, pair))
    partner = (pair, mirror)
    inner = lax.rem((chip + 1) // 2, 2)
    low = chip < 2
    is_inner = inner == 1
    not_ = jnp.logical_not

    def at(chip, core):
        return {"seq": x * GROUP + chip * 2 + core}

    def in_group(k):
        rank = lax.rem(me + k, GROUP)
        return rank, {"seq": x * GROUP + rank}

    leads = me == 0
    group_at = x + x_count * doc
    stages = (x_count * z_count).bit_length() - 1

    def gate_partner(stage):
        bit = 1 << stage
        other = group_at + bit - 2 * bit * lax.rem(group_at // bit, 2)
        return {"seq": lax.rem(other, x_count) * GROUP, "doc": other // x_count}

    barrier = pltpu.get_barrier_semaphore()

    def greet(device):
        pl.semaphore_signal(barrier, inc=1, device_id=device, device_id_type=MESH)

    def greet_group(k, c):
        greet(in_group(k)[1])
        return c

    lax.fori_loop(1, GROUP, greet_group, 0)

    @pl.when(leads)
    def _():
        for stage in range(stages):
            greet(gate_partner(stage))


    def send(src, dst, send_sem, recv_sem, device):
        pltpu.make_async_remote_copy(
            src_ref=src, dst_ref=dst, send_sem=send_sem, recv_sem=recv_sem,
            device_id=device, device_id_type=MESH,
        ).start()

    def await_bytes(ref, sem):
        pltpu.make_async_copy(ref, ref, sem).wait()

    def here(job):
        return pl.ds(HERE[job] * E, HEADS[job] * E)

    def first_head(job, chip, core):
        plan = chip // 2 if job == A else lax.rem((chip + 1) // 2, 2)
        return THERE[job] + (plan * 2 + core) * HEADS[job]

    def there(job, chip, core):
        return pl.ds(pl.multiple_of(first_head(job, chip, core) * E, E), HEADS[job] * E)

    def place(job, chip):
        return chip // 2 if job == A else lax.rem(chip, 2)

    def rows_at(block, core):
        return pl.ds(pl.multiple_of(block * BLOCK + core * ROWS, ROWS), ROWS)

    K, V, LATS, COT, QC, Q = range(6)
    refs = (k_ref, v_ref, lat_ref, cot_ref, qc_ref, q_ref)
    bufs = (k_buf, v_buf, lat_buf, cot_buf, qc_buf, q_buf)

    def in_views(t, job, to_chip, to_core):
        cols = there(job, to_chip, to_core)
        if t == LATS:
            return lat_ref.at[0, 0, :, :, cols], lat_buf.at[me, :, :, here(job)]
        rows = rows_at(chip, core) if t in (K, V) else rows_at(place(job, chip), core)
        return refs[t].at[0, :, cols], bufs[t].at[rows, here(job)]

    gate_load = pltpu.make_async_copy(gate_ref, gate_buf, gate_sem)
    gate_load.start()
    pltpu.make_async_copy(media_ref, media_buf.at[me], media_recv).start()
    for t in (LATS, K, V, COT, QC, Q):
        for job in (A, B):
            src, dst = in_views(t, job, chip, core)
            pltpu.make_async_copy(src, dst, in_recv.at[job, t]).start()

    @pl.when(leads)
    def _():
        pl.semaphore_wait(barrier, GROUP - 1 + stages)

    @pl.when(not_(leads))
    def _():
        pl.semaphore_wait(barrier, GROUP - 1)

    def send_in(t, job):
        for to_chip, to_core in ((homes[job][1], core), (homes[job][1], 1 - core), (chip, 1 - core)):
            src, dst = in_views(t, job, to_chip, to_core)
            send(src, dst, in_send.at[job, t], in_recv.at[job, t], at(to_chip, to_core))

    def send_media(k, c):
        send(media_ref, media_buf.at[me], media_send, media_recv, in_group(k)[1])
        return c

    for t in (LATS, K, V, COT, QC, Q):
        send_in(t, A)
        if t != Q:
            send_in(t, B)
        if t == LATS:
            lax.fori_loop(1, GROUP, send_media, 0)

    def await_in(t, job):
        if t == LATS:
            await_bytes(lat_buf.at[pl.ds(0, 4), :, :, here(job)], in_recv.at[job, t])
        else:
            await_bytes(q_buf.at[:, here(job)], in_recv.at[job, t])

    def pass_on(job, t, first, count):
        part = bufs[t].at[pl.ds(first, count), :, :, here(job)] if t == LATS else bufs[t].at[pl.ds(first, count), here(job)]
        send(part, part, pass_send.at[job, t], pass_recv.at[job, t], at(partner[job], core))

    for job in (A, B):
        await_in(LATS, job)
    pl.when(not_(is_inner))(lambda: (pass_on(A, LATS, 0, 2), pass_on(A, LATS, 6, 2)) and None)
    pl.when(is_inner)(lambda: pass_on(A, LATS, 2, 4))
    pl.when(low)(lambda: pass_on(B, LATS, 0, 4))
    pl.when(not_(low))(lambda: pass_on(B, LATS, 4, 4))
    for t in (K, V):
        for job in (A, B):
            await_in(t, job)
        pl.when(not_(is_inner))(lambda: pass_on(A, t, 0, BLOCK))
        pl.when(is_inner)(lambda: pass_on(A, t, BLOCK, 2 * BLOCK))
        pl.when(low)(lambda: pass_on(B, t, 0, 2 * BLOCK))
    send_in(Q, B)

    OUT, GQ, GQC, GK, GV, GLAT = range(6)
    out_refs = (out_ref, gq_ref, gqc_ref, gk_ref, gv_ref, glat_ref)
    out_bufs = (out_buf, gq_buf, gqc_buf, gk_buf, gv_buf, glat_buf)

    def out_views(t, job, to_chip, to_core, first, count):
        near = pl.ds((HERE[job] + first) * E, count * E)
        far = pl.ds(pl.multiple_of((first_head(job, chip, core) + first) * E, E), count * E)
        if t == GLAT:
            return glat_buf.at[to_chip * 2 + to_core, :, :, near], glat_ref.at[0, 0, :, :, far]
        rows = rows_at(to_chip, to_core) if t in (GK, GV) else rows_at(place(job, to_chip), to_core)
        return out_bufs[t].at[rows, near], out_refs[t].at[0, :, far]

    def send_home(job, part, first=0, count=None):
        count = count or HEADS[job]
        for t in part:
            src, dst = out_views(t, job, chip, core, first, count)
            pltpu.make_async_copy(src, dst, out_recv.at[t]).start()
            for to_chip, to_core in ((homes[job][1], core), (homes[job][1], 1 - core), (chip, 1 - core)):
                src, dst = out_views(t, job, to_chip, to_core, first, count)
                send(src, dst, out_send.at[job, t], out_recv.at[t], at(to_chip, to_core))

    await_bytes(media_buf, media_recv)
    gate_load.wait()
    first_slot = x * GROUP

    def send_glat(job, first, count):
        send(
            glat_buf.at[pl.ds(first, count), :, :, here(job)], glat_in.at[pl.ds(first, count), :, :, here(job)],
            part_send.at[job, 2], part_recv.at[job, 2], at(partner[job], core),
        )

    for job in (A, B):
        await_in(COT, job)
        await_in(QC, job)
        await_bytes(lat_buf.at[pl.ds(0, 4), :, :, here(job)], pass_recv.at[job, LATS])
        head_of = first_head(job, chip, core)

        def media_row(i, job=job):
            block = (3 * i * (1 - inner) + (1 + i) * inner) if job == A else 2 * (chip // 2) + i
            cited = jnp.concatenate([media_buf[2 * block], media_buf[2 * block + 1]], axis=1)
            return jnp.where(cited >= 0, cited - first_slot, -1)

        def cross_step(head, c, job=job, head_of=head_of, media_row=media_row):
            gate_own[pl.ds(HERE[job] + head, 1), :] = cross_head(
                head_cols(job, head), gate_buf[pl.ds(head_of + head, 1), :], media_row,
                qc_buf, cot_buf, lat_buf, mixed, gqc_buf, glat_buf,
            )
            return c

        lax.fori_loop(0, HEADS[job], cross_step, 0)
        if job == B:
            gate_all[me] = gate_own[...]

            @pl.when(not_(leads))
            def _():
                send(gate_own, gate_all.at[me], gate_send.at[stages], gather_recv.at[me], {"seq": x * GROUP})

        if job == A:
            pl.when(not_(is_inner))(lambda: send_glat(A, 2, 4))
            pl.when(is_inner)(lambda: (send_glat(A, 0, 2), send_glat(A, 6, 2)) and None)
        else:
            pl.when(low)(lambda: send_glat(B, 4, 4))
            pl.when(not_(low))(lambda: send_glat(B, 0, 4))
        send_home(job, (GQC,))

    def send_part(job, first_row, row_count, first, count):
        rows, cols = pl.ds(first_row, row_count), pl.ds((HERE[job] + first) * E, count * E)
        for t, (buf, into) in enumerate(((gk_buf, gk_in), (gv_buf, gv_in))):
            send(buf.at[rows, cols], into.at[rows, cols], part_send.at[job, t], part_recv.at[job, t], at(partner[job], core))

    for job in (A, B):
        await_in(Q, job)
        for t in (K, V):
            if job == A:
                pl.when(not_(is_inner))(lambda: await_bytes(k_buf.at[pl.ds(0, 2 * BLOCK), here(A)], pass_recv.at[A, t]))
                pl.when(is_inner)(lambda: await_bytes(k_buf.at[pl.ds(0, BLOCK), here(A)], pass_recv.at[A, t]))
            else:
                pl.when(not_(low))(lambda: await_bytes(k_buf.at[pl.ds(0, 2 * BLOCK), here(B)], pass_recv.at[B, t]))

        def self_step(head, c, job=job):
            cols = head_cols(job, head)
            acc_k[...] = jnp.zeros((DOC, E), F32)
            acc_v[...] = jnp.zeros((DOC, E), F32)

            def block(i):
                self_block(
                    i, place(job, i) if job == A else i % 2, cols,
                    q_buf, k_buf, v_buf, cot_buf, mixed, out_buf, gq_buf, acc_k, acc_v,
                )

            if job == A:
                pl.when(not_(is_inner))(lambda: (block(0), block(3)) and None)
                pl.when(is_inner)(lambda: (block(1), block(2)) and None)
            else:
                pl.when(low)(lambda: (block(0), block(1)) and None)
                pl.when(not_(low))(lambda: (block(2), block(3)) and None)
            gk_buf[:, cols] = (SCALE * acc_k[...]).astype(BF16)
            gv_buf[:, cols] = acc_v[...].astype(BF16)
            for first, count in BATCHES[job]:

                @pl.when(head == first + count - 1)
                def _(first=first, count=count):
                    if job == A:
                        pl.when(not_(is_inner))(lambda: send_part(A, BLOCK, 2 * BLOCK, first, count))
                        pl.when(is_inner)(lambda: send_part(A, 0, BLOCK, first, count))
                    else:
                        pl.when(not_(low))(lambda: send_part(B, 0, 2 * BLOCK, first, count))
                    send_home(job, (OUT, GQ), first, count)

            return c

        lax.fori_loop(0, HEADS[job], self_step, 0)

    def add(buf, into, *where):
        buf[where] = (buf[where].astype(F32) + into[where].astype(F32)).astype(BF16)

    def add_glat(job, first, count):
        add(glat_buf, glat_in, pl.ds(first, count), slice(None), slice(None), here(job))

    def add_part(job, t, first, count):
        buf, into = ((gk_buf, gk_in), (gv_buf, gv_in))[t]
        await_bytes(into.at[pl.ds(first, count), here(job)], part_recv.at[job, t])
        add(buf, into, pl.ds(first, count), here(job))

    def finish_glat(job):
        await_bytes(glat_in.at[pl.ds(0, 4), :, :, here(job)], part_recv.at[job, 2])
        if job == A:
            pl.when(not_(is_inner))(lambda: (add_glat(A, 0, 2), add_glat(A, 6, 2)) and None)
            pl.when(is_inner)(lambda: add_glat(A, 2, 4))
        else:
            pl.when(low)(lambda: add_glat(B, 0, 4))
            pl.when(not_(low))(lambda: add_glat(B, 4, 4))
        send_home(job, (GLAT,))

    def finish_part(job):
        for t, result in enumerate((GK, GV)):
            if job == A:
                pl.when(not_(is_inner))(lambda: add_part(A, t, 0, BLOCK))
                pl.when(is_inner)(lambda: add_part(A, t, BLOCK, 2 * BLOCK))
            else:
                pl.when(low)(lambda: add_part(B, t, 0, 2 * BLOCK))
            send_home(job, (result,))

    def gate_copy(stage):
        return pltpu.make_async_remote_copy(
            src_ref=gate_sums.at[stage], dst_ref=gate_in.at[stage],
            send_sem=gate_send.at[stage], recv_sem=gate_recv.at[stage],
            device_id=gate_partner(stage), device_id_type=MESH,
        )

    def gate_stage(stage):
        @pl.when(leads)
        def _():
            if stage == 0:
                def gathered(rank, c):
                    await_bytes(gate_all.at[rank], gather_recv.at[rank])
                    return c

                lax.fori_loop(1, GROUP, gathered, 0)
                gate_sums[0] = gate_all[...]
            else:
                gate_copy(stage - 1).wait()
                gate_sums[stage] = gate_sums[stage - 1] + gate_in[stage - 1]
            if stage < stages:
                gate_copy(stage).start()
            else:
                def spread(k, c):
                    send(
                        gate_sums.at[stages], gate_sums.at[stages], spread_send.at[k], gate_recv.at[stages],
                        {"seq": x * GROUP + k},
                    )
                    return c

                lax.fori_loop(1, GROUP, spread, 0)

    gate_stage(0)
    finish_glat(A)
    gate_stage(1)
    finish_glat(B)
    gate_stage(2)
    finish_part(B)
    for stage in range(3, stages):
        gate_stage(stage)
    finish_part(A)
    gate_stage(stages)

    @pl.when(leads)
    def _():
        def spread_end(k, c):
            await_bytes(gate_sums.at[stages], spread_send.at[k])
            return c

        lax.fori_loop(1, GROUP, spread_end, 0)

    @pl.when(not_(leads))
    def _():
        await_bytes(gate_own, gate_send.at[stages])
        await_bytes(gate_sums.at[stages], gate_recv.at[stages])

    for job, owners in ((A, ((0, 1), (2, 3))), (B, ((0, 3), (1, 2)))):
        part = pl.ds(HERE[job], HEADS[job])
        for plan, (one, two) in enumerate(owners):
            for side in range(2):
                first = THERE[job] + (plan * 2 + side) * HEADS[job]
                gate_out_ref[pl.ds(first, HEADS[job]), :] = (
                    gate_sums[stages, one * 2 + side, part, :] + gate_sums[stages, two * 2 + side, part, :]
                )

    await_bytes(media_buf.at[pl.ds(0, GROUP - 1)], media_send)
    for job in (A, B):
        for t in range(6):
            sent = lat_buf.at[pl.ds(0, 3), :, :, here(job)] if t == LATS else q_buf.at[pl.ds(0, 3 * ROWS), here(job)]
            await_bytes(sent, in_send.at[job, t])
            sent = glat_buf.at[pl.ds(0, 3), :, :, here(job)] if t == GLAT else out_buf.at[pl.ds(0, 3 * ROWS), here(job)]
            await_bytes(sent, out_send.at[job, t])
        await_bytes(lat_buf.at[pl.ds(0, 4), :, :, here(job)], pass_send.at[job, LATS])
        await_bytes(glat_buf.at[pl.ds(0, 4), :, :, here(job)], part_send.at[job, 2])

    def sent_rows(job, rows, pass_only, part_only):
        for t in (0, 1):
            if pass_only:
                await_bytes(k_buf.at[pl.ds(0, rows), here(job)], pass_send.at[job, t])
            if part_only:
                await_bytes(gk_buf.at[pl.ds(0, rows), here(job)], part_send.at[job, t])

    @pl.when(is_inner)
    def _():
        sent_rows(A, 2 * BLOCK, True, False)
        sent_rows(A, BLOCK, False, True)

    @pl.when(not_(is_inner))
    def _():
        sent_rows(A, BLOCK, True, False)
        sent_rows(A, 2 * BLOCK, False, True)

    pl.when(low)(lambda: sent_rows(B, 2 * BLOCK, True, False))
    pl.when(not_(low))(lambda: sent_rows(B, 2 * BLOCK, False, True))
    for t in range(6):
        await_bytes(out_refs[t], out_recv.at[t])


def finish_kernel(*refs):
    count = len(refs) // 2
    sems = refs[-1]
    copies = [pltpu.make_async_copy(refs[i], refs[count + i], sems.at[i]) for i in range(count)]
    for copy in copies:
        copy.start()
    for copy in copies:
        copy.wait()


def per_device(x_count, z_count, q, k, v, qc, lat, media, gate, cot):
    anywhere = pl.BlockSpec(memory_space=pl.ANY)
    vmem = pl.BlockSpec(memory_space=pltpu.VMEM)
    token = jax.ShapeDtypeStruct((1, ROWS, WIDTH), BF16)
    gate_shape = (ALL_HEADS, E)
    stages = (x_count * z_count).bit_length() - 1
    outs = (token,) * 5 + (jax.ShapeDtypeStruct(lat.shape, BF16), jax.ShapeDtypeStruct(gate_shape, F32))
    queries = pltpu.VMEM((2 * BLOCK, COLS), BF16)
    tokens = pltpu.VMEM((DOC, COLS), BF16)
    latents = pltpu.VMEM((GROUP, 2, LAT, COLS), BF16)
    dma = pltpu.SemaphoreType.DMA
    results = pl.pallas_call(
        functools.partial(kernel, x_count, z_count),
        name="attention",
        out_shape=outs,
        in_specs=[anywhere] * 8,
        out_specs=[anywhere] * 6 + [vmem],
        scratch_shapes=[
            queries, queries, queries, tokens, tokens, latents, pltpu.VMEM((GROUP, 1, ROWS), jnp.int32),
            queries, queries, queries, tokens, tokens, latents, tokens, tokens, latents,
            pltpu.VMEM((2 * BLOCK, COLS), F32), pltpu.VMEM((DOC, E), F32), pltpu.VMEM((DOC, E), F32),
            pltpu.VMEM(gate_shape, F32), pltpu.VMEM((8, E), F32), pltpu.VMEM((GROUP, 8, E), F32),
            pltpu.VMEM((stages + 1, GROUP, 8, E), F32), pltpu.VMEM((stages, GROUP, 8, E), F32),
            dma(()), dma(()), dma(()), dma((2, 6)), dma((2, 6)), dma((2, 3)), dma((2, 3)), dma((2, 3)), dma((2, 3)),
            dma((2, 6)), dma((6,)), dma((GROUP,)), dma((stages + 1,)), dma((stages + 1,)), dma((GROUP,)),
        ],
        compiler_params=pltpu.CompilerParams(
            collective_id=0, has_side_effects=True, vmem_limit_bytes=95 << 19
        ),
    )(q, k, v, qc, lat, cot, media, gate.reshape(gate_shape))
    done = pl.pallas_call(
        finish_kernel,
        name="finish",
        out_shape=outs,
        in_specs=[vmem] * 7,
        out_specs=[anywhere] * 7,
        scratch_shapes=[dma((7,))],
        compiler_params=pltpu.CompilerParams(vmem_limit_bytes=47 << 20),
    )(*results)
    return (*done[:6], done[6].reshape(WIDTH))


def solution(mesh):
    token = P("doc", "seq", None)
    latent = P("doc", "seq", None, None, None)
    return jax.shard_map(
        functools.partial(per_device, mesh.shape["seq"] // GROUP, mesh.shape["doc"]),
        mesh=mesh,
        in_specs=(token, token, token, token, latent, P("doc", "seq"), P(), token),
        out_specs=(token, token, token, token, token, latent, P()),
        check_vma=False,
    )
```

```python
import functools

import jax
import jax.numpy as jnp
from jax import lax
from jax.experimental import pallas as pl
from jax.experimental.pallas import tpu as pltpu
from jax.sharding import PartitionSpec as P

E = 128
LAT = 64
GROUP = 8
ROWS = 128
BLOCK = 256
DOC = GROUP * ROWS
KEYS = GROUP * LAT
A, B = 0, 1
HEADS = (5, 3)
BATCHES = (((0, 1), (1, 2), (3, 2)), ((0, 3),))
HERE = (0, 5)
THERE = (0, 20)
ALL_HEADS = 32
WIDTH = ALL_HEADS * E
COLS = sum(HEADS) * E
SCALE = E**-0.5
NEG_FILL = -1e30
MESH = pl.DeviceIdType.MESH
F32 = jnp.float32
BF16 = jnp.bfloat16


def dot(left, right, left_dim, right_dim):
    return lax.dot_general(
        left, right, (((left_dim,), (right_dim,)), ((), ())), preferred_element_type=F32
    )


def softmax_and_grad(scores, weights_grad_of, inverse_of):
    peak = jnp.max(scores, axis=0, keepdims=True)
    weights = jnp.exp(SCALE * (scores - peak))
    weights = weights * inverse_of(jnp.sum(weights, axis=0, keepdims=True))
    half = weights.astype(BF16)
    weights_grad = weights_grad_of()
    inner = jnp.sum(weights * weights_grad, axis=0, keepdims=True)
    return half, (weights * (weights_grad - inner)).astype(BF16)


def head_cols(job, head):
    return pl.ds(pl.multiple_of((HERE[job] + head) * E, E), E)


def cross_head(cols, gate_row, media_row, qc_buf, cot_buf, lat_buf, mixed, gqc_buf, glat_buf):
    keys = lat_buf[:, 0, :, cols].reshape(KEYS, E)
    values = lat_buf[:, 1, :, cols].reshape(KEYS, E)
    tanh_gate = jnp.tanh(gate_row)
    slot = lax.broadcasted_iota(jnp.int32, (KEYS, BLOCK), 0) // LAT
    gate_sum = jnp.zeros((1, E), F32)
    keys_grad = jnp.zeros((KEYS, E), F32)
    values_grad = jnp.zeros((KEYS, E), F32)
    for i in range(2):
        rows = pl.ds(i * BLOCK, BLOCK)
        cited = media_row(i)
        queries = qc_buf[rows, cols]
        cot = cot_buf[rows, cols].astype(F32)
        cot_cross = (cot * tanh_gate).astype(BF16)
        scores = dot(keys, queries, 1, 1)
        scores = jnp.where(slot == cited, scores, NEG_FILL)
        half, scores_grad = softmax_and_grad(
            scores,
            lambda: dot(values, cot_cross, 1, 1),
            lambda total: jnp.where(cited >= 0, 1.0 / total, 0.0),
        )
        out = dot(values, half, 0, 0).T
        mixed[rows, cols] = tanh_gate * out
        values_grad += dot(half, cot_cross, 1, 0)
        gqc_buf[rows, cols] = (SCALE * dot(keys, scores_grad, 0, 0)).T.astype(BF16)
        keys_grad += dot(scores_grad, queries, 1, 0)
        gate_sum += jnp.sum(cot * out, axis=0, keepdims=True)
    glat_buf[:, 0, :, cols] = (SCALE * keys_grad).astype(BF16).reshape(GROUP, LAT, E)
    glat_buf[:, 1, :, cols] = values_grad.astype(BF16).reshape(GROUP, LAT, E)
    return gate_sum * (1.0 - tanh_gate * tanh_gate)


def self_block(i, place, cols, q_buf, k_buf, v_buf, cot_buf, mixed, out_buf, gq_buf, acc_k, acc_v):
    rows = pl.ds(place * BLOCK, BLOCK)
    seen = pl.ds(0, (i + 1) * BLOCK)
    queries = q_buf[rows, cols]
    cot = cot_buf[rows, cols]
    keys = k_buf[seen, cols]
    values = v_buf[seen, cols]
    scores = dot(keys, queries, 1, 1)
    shape = scores.shape
    causal = lax.broadcasted_iota(jnp.int32, shape, 0) <= i * BLOCK + lax.broadcasted_iota(jnp.int32, shape, 1)
    scores = jnp.where(causal, scores, -jnp.inf)
    half, scores_grad = softmax_and_grad(
        scores, lambda: dot(values, cot, 1, 1), lambda total: 1.0 / total
    )
    out = dot(values, half, 0, 0).T
    out_buf[rows, cols] = (out + mixed[rows, cols]).astype(BF16)
    acc_v[seen, :] += dot(half, cot, 1, 0)
    gq_buf[rows, cols] = (SCALE * dot(keys, scores_grad, 0, 0)).T.astype(BF16)
    acc_k[seen, :] += dot(scores_grad, queries, 1, 0)


def kernel(
    x_count, z_count,
    q_ref, k_ref, v_ref, qc_ref, lat_ref, cot_ref, media_ref, gate_ref,
    out_ref, gq_ref, gk_ref, gv_ref, gqc_ref, glat_ref, gate_out_ref,
    q_buf, qc_buf, cot_buf, k_buf, v_buf, lat_buf, media_buf,
    out_buf, gq_buf, gqc_buf, gk_buf, gv_buf, glat_buf, gk_in, gv_in, glat_in,
    mixed, acc_k, acc_v, gate_buf, gate_own, gate_all, gate_sums, gate_in,
    gate_sem, media_send, media_recv, in_send, in_recv, pass_send, pass_recv, part_send, part_recv,
    out_send, out_recv, gather_recv, gate_send, gate_recv, spread_send,
):
    seq = lax.axis_index("seq")
    doc = lax.axis_index("doc")
    x = seq // GROUP
    me = lax.rem(seq, GROUP)
    chip = me // 2
    core = lax.rem(me, 2)
    mirror = 3 - chip
    pair = chip + 1 - 2 * lax.rem(chip, 2)
    homes = ((chip, mirror), (chip, pair))
    partner = (pair, mirror)
    inner = lax.rem((chip + 1) // 2, 2)
    low = chip < 2
    is_inner = inner == 1
    not_ = jnp.logical_not

    def at(chip, core):
        return {"seq": x * GROUP + chip * 2 + core}

    def in_group(k):
        rank = lax.rem(me + k, GROUP)
        return rank, {"seq": x * GROUP + rank}

    leads = me == 0
    group_at = x + x_count * doc
    stages = (x_count * z_count).bit_length() - 1

    def gate_partner(stage):
        bit = 1 << stage
        other = group_at + bit - 2 * bit * lax.rem(group_at // bit, 2)
        return {"seq": lax.rem(other, x_count) * GROUP, "doc": other // x_count}

    barrier = pltpu.get_barrier_semaphore()

    def greet(device):
        pl.semaphore_signal(barrier, inc=1, device_id=device, device_id_type=MESH)

    def greet_group(k, c):
        greet(in_group(k)[1])
        return c

    lax.fori_loop(1, GROUP, greet_group, 0)

    @pl.when(leads)
    def _():
        for stage in range(stages):
            greet(gate_partner(stage))


    def send(src, dst, send_sem, recv_sem, device):
        pltpu.make_async_remote_copy(
            src_ref=src, dst_ref=dst, send_sem=send_sem, recv_sem=recv_sem,
            device_id=device, device_id_type=MESH,
        ).start()

    def await_bytes(ref, sem):
        pltpu.make_async_copy(ref, ref, sem).wait()

    def here(job):
        return pl.ds(HERE[job] * E, HEADS[job] * E)

    def first_head(job, chip, core):
        plan = chip // 2 if job == A else lax.rem((chip + 1) // 2, 2)
        return THERE[job] + (plan * 2 + core) * HEADS[job]

    def there(job, chip, core):
        return pl.ds(pl.multiple_of(first_head(job, chip, core) * E, E), HEADS[job] * E)

    def place(job, chip):
        return chip // 2 if job == A else lax.rem(chip, 2)

    def rows_at(block, core):
        return pl.ds(pl.multiple_of(block * BLOCK + core * ROWS, ROWS), ROWS)

    K, V, LATS, COT, QC, Q = range(6)
    refs = (k_ref, v_ref, lat_ref, cot_ref, qc_ref, q_ref)
    bufs = (k_buf, v_buf, lat_buf, cot_buf, qc_buf, q_buf)

    def in_views(t, job, to_chip, to_core):
        cols = there(job, to_chip, to_core)
        if t == LATS:
            return lat_ref.at[0, 0, :, :, cols], lat_buf.at[me, :, :, here(job)]
        rows = rows_at(chip, core) if t in (K, V) else rows_at(place(job, chip), core)
        return refs[t].at[0, :, cols], bufs[t].at[rows, here(job)]

    gate_load = pltpu.make_async_copy(gate_ref, gate_buf.at[pl.ds(0, ALL_HEADS)], gate_sem)
    gate_load.start()
    pltpu.make_async_copy(media_ref, media_buf.at[me], media_recv).start()
    for t in (LATS, K, V, COT, QC, Q):
        for job in (A, B):
            src, dst = in_views(t, job, chip, core)
            pltpu.make_async_copy(src, dst, in_recv.at[job, t]).start()

    @pl.when(leads)
    def _():
        pl.semaphore_wait(barrier, GROUP - 1 + stages)

    @pl.when(not_(leads))
    def _():
        pl.semaphore_wait(barrier, GROUP - 1)

    def send_in(t, job):
        for to_chip, to_core in ((homes[job][1], core), (homes[job][1], 1 - core), (chip, 1 - core)):
            src, dst = in_views(t, job, to_chip, to_core)
            send(src, dst, in_send.at[job, t], in_recv.at[job, t], at(to_chip, to_core))

    def send_media(k, c):
        send(media_ref, media_buf.at[me], media_send, media_recv, in_group(k)[1])
        return c

    for t in (LATS, K, V, COT, QC, Q):
        send_in(t, A)
        if t != Q:
            send_in(t, B)
        if t == LATS:
            lax.fori_loop(1, GROUP, send_media, 0)

    def await_in(t, job):
        if t == LATS:
            await_bytes(lat_buf.at[pl.ds(0, 4), :, :, here(job)], in_recv.at[job, t])
        else:
            await_bytes(q_buf.at[:, here(job)], in_recv.at[job, t])

    def pass_on(job, t, first, count):
        part = bufs[t].at[pl.ds(first, count), :, :, here(job)] if t == LATS else bufs[t].at[pl.ds(first, count), here(job)]
        send(part, part, pass_send.at[job, t], pass_recv.at[job, t], at(partner[job], core))

    for job in (A, B):
        await_in(LATS, job)
    pl.when(not_(is_inner))(lambda: (pass_on(A, LATS, 0, 2), pass_on(A, LATS, 6, 2)) and None)
    pl.when(is_inner)(lambda: pass_on(A, LATS, 2, 4))
    pl.when(low)(lambda: pass_on(B, LATS, 0, 4))
    pl.when(not_(low))(lambda: pass_on(B, LATS, 4, 4))
    for t in (K, V):
        for job in (A, B):
            await_in(t, job)
        pl.when(not_(is_inner))(lambda: pass_on(A, t, 0, BLOCK))
        pl.when(is_inner)(lambda: pass_on(A, t, BLOCK, 2 * BLOCK))
        pl.when(low)(lambda: pass_on(B, t, 0, 2 * BLOCK))
    send_in(Q, B)

    OUT, GQ, GQC, GK, GV, GLAT = range(6)
    out_refs = (out_ref, gq_ref, gqc_ref, gk_ref, gv_ref, glat_ref)
    out_bufs = (out_buf, gq_buf, gqc_buf, gk_buf, gv_buf, glat_buf)

    def out_views(t, job, to_chip, to_core, first, count):
        near = pl.ds((HERE[job] + first) * E, count * E)
        far = pl.ds(pl.multiple_of((first_head(job, chip, core) + first) * E, E), count * E)
        if t == GLAT:
            return glat_buf.at[to_chip * 2 + to_core, :, :, near], glat_ref.at[0, 0, :, :, far]
        rows = rows_at(to_chip, to_core) if t in (GK, GV) else rows_at(place(job, to_chip), to_core)
        return out_bufs[t].at[rows, near], out_refs[t].at[0, :, far]

    def send_home(job, part, first=0, count=None):
        count = count or HEADS[job]
        for t in part:
            src, dst = out_views(t, job, chip, core, first, count)
            pltpu.make_async_copy(src, dst, out_recv.at[t]).start()
            for to_chip, to_core in ((homes[job][1], core), (homes[job][1], 1 - core), (chip, 1 - core)):
                src, dst = out_views(t, job, to_chip, to_core, first, count)
                send(src, dst, out_send.at[job, t], out_recv.at[t], at(to_chip, to_core))

    await_bytes(media_buf, media_recv)
    gate_load.wait()
    first_slot = x * GROUP

    def send_glat(job, first, count):
        send(
            glat_buf.at[pl.ds(first, count), :, :, here(job)], glat_in.at[pl.ds(first, count), :, :, here(job)],
            part_send.at[job, 2], part_recv.at[job, 2], at(partner[job], core),
        )

    for job in (A, B):
        await_in(COT, job)
        await_in(QC, job)
        await_bytes(lat_buf.at[pl.ds(0, 4), :, :, here(job)], pass_recv.at[job, LATS])
        head_of = first_head(job, chip, core)

        def media_row(i, job=job):
            block = (3 * i * (1 - inner) + (1 + i) * inner) if job == A else 2 * (chip // 2) + i
            cited = jnp.concatenate([media_buf[2 * block], media_buf[2 * block + 1]], axis=1)
            return jnp.where(cited >= 0, cited - first_slot, -1)

        def cross_step(head, c, job=job, head_of=head_of, media_row=media_row):
            gate_own[pl.ds(HERE[job] + head, 1), :] = cross_head(
                head_cols(job, head), gate_buf[pl.ds(head_of + head, 1), :], media_row,
                qc_buf, cot_buf, lat_buf, mixed, gqc_buf, glat_buf,
            )
            return c

        lax.fori_loop(0, HEADS[job], cross_step, 0)
        if job == B:
            gate_all[me] = gate_own[pl.ds(0, 8), :]

            @pl.when(not_(leads))
            def _():
                send(gate_own.at[pl.ds(0, 8)], gate_all.at[me], gate_send.at[stages], gather_recv.at[me], {"seq": x * GROUP})

        if job == A:
            pl.when(not_(is_inner))(lambda: send_glat(A, 2, 4))
            pl.when(is_inner)(lambda: (send_glat(A, 0, 2), send_glat(A, 6, 2)) and None)
        else:
            pl.when(low)(lambda: send_glat(B, 4, 4))
            pl.when(not_(low))(lambda: send_glat(B, 0, 4))
        send_home(job, (GQC,))

    def send_part(job, first_row, row_count, first, count):
        rows, cols = pl.ds(first_row, row_count), pl.ds((HERE[job] + first) * E, count * E)
        for t, (buf, into) in enumerate(((gk_buf, gk_in), (gv_buf, gv_in))):
            send(buf.at[rows, cols], into.at[rows, cols], part_send.at[job, t], part_recv.at[job, t], at(partner[job], core))

    for job in (A, B):
        await_in(Q, job)
        for t in (K, V):
            if job == A:
                pl.when(not_(is_inner))(lambda: await_bytes(k_buf.at[pl.ds(0, 2 * BLOCK), here(A)], pass_recv.at[A, t]))
                pl.when(is_inner)(lambda: await_bytes(k_buf.at[pl.ds(0, BLOCK), here(A)], pass_recv.at[A, t]))
            else:
                pl.when(not_(low))(lambda: await_bytes(k_buf.at[pl.ds(0, 2 * BLOCK), here(B)], pass_recv.at[B, t]))

        def self_step(head, c, job=job):
            cols = head_cols(job, head)
            acc_k[...] = jnp.zeros((DOC, E), F32)
            acc_v[...] = jnp.zeros((DOC, E), F32)

            def block(i):
                self_block(
                    i, place(job, i) if job == A else i % 2, cols,
                    q_buf, k_buf, v_buf, cot_buf, mixed, out_buf, gq_buf, acc_k, acc_v,
                )

            if job == A:
                pl.when(not_(is_inner))(lambda: (block(0), block(3)) and None)
                pl.when(is_inner)(lambda: (block(1), block(2)) and None)
            else:
                pl.when(low)(lambda: (block(0), block(1)) and None)
                pl.when(not_(low))(lambda: (block(2), block(3)) and None)
            gk_buf[:, cols] = (SCALE * acc_k[...]).astype(BF16)
            gv_buf[:, cols] = acc_v[...].astype(BF16)
            for first, count in BATCHES[job]:

                @pl.when(head == first + count - 1)
                def _(first=first, count=count):
                    if job == A:
                        pl.when(not_(is_inner))(lambda: send_part(A, BLOCK, 2 * BLOCK, first, count))
                        pl.when(is_inner)(lambda: send_part(A, 0, BLOCK, first, count))
                    else:
                        pl.when(not_(low))(lambda: send_part(B, 0, 2 * BLOCK, first, count))
                    send_home(job, (OUT, GQ), first, count)

            return c

        lax.fori_loop(0, HEADS[job], self_step, 0)

    def add(buf, into, *where):
        buf[where] = (buf[where].astype(F32) + into[where].astype(F32)).astype(BF16)

    def add_glat(job, first, count):
        add(glat_buf, glat_in, pl.ds(first, count), slice(None), slice(None), here(job))

    def add_part(job, t, first, count):
        buf, into = ((gk_buf, gk_in), (gv_buf, gv_in))[t]
        await_bytes(into.at[pl.ds(first, count), here(job)], part_recv.at[job, t])
        add(buf, into, pl.ds(first, count), here(job))

    def finish_glat(job):
        await_bytes(glat_in.at[pl.ds(0, 4), :, :, here(job)], part_recv.at[job, 2])
        if job == A:
            pl.when(not_(is_inner))(lambda: (add_glat(A, 0, 2), add_glat(A, 6, 2)) and None)
            pl.when(is_inner)(lambda: add_glat(A, 2, 4))
        else:
            pl.when(low)(lambda: add_glat(B, 0, 4))
            pl.when(not_(low))(lambda: add_glat(B, 4, 4))
        send_home(job, (GLAT,))

    def finish_part(job):
        for t, result in enumerate((GK, GV)):
            if job == A:
                pl.when(not_(is_inner))(lambda: add_part(A, t, 0, BLOCK))
                pl.when(is_inner)(lambda: add_part(A, t, BLOCK, 2 * BLOCK))
            else:
                pl.when(low)(lambda: add_part(B, t, 0, 2 * BLOCK))
            send_home(job, (result,))

    def gate_copy(stage):
        return pltpu.make_async_remote_copy(
            src_ref=gate_sums.at[stage], dst_ref=gate_in.at[stage],
            send_sem=gate_send.at[stage], recv_sem=gate_recv.at[stage],
            device_id=gate_partner(stage), device_id_type=MESH,
        )

    def gate_stage(stage):
        @pl.when(leads)
        def _():
            if stage == 0:
                def gathered(rank, c):
                    await_bytes(gate_all.at[rank], gather_recv.at[rank])
                    return c

                lax.fori_loop(1, GROUP, gathered, 0)
                gate_sums[0] = gate_all[...]
            else:
                gate_copy(stage - 1).wait()
                gate_sums[stage] = gate_sums[stage - 1] + gate_in[stage - 1]
            if stage < stages:
                gate_copy(stage).start()
            else:
                def spread(k, c):
                    send(
                        gate_sums.at[stages], gate_sums.at[stages], spread_send.at[k], gate_recv.at[stages],
                        {"seq": x * GROUP + k},
                    )
                    return c

                lax.fori_loop(1, GROUP, spread, 0)

    gate_stage(0)
    finish_glat(A)
    gate_stage(1)
    finish_glat(B)
    gate_stage(2)
    finish_part(B)
    for stage in range(3, stages):
        gate_stage(stage)
    finish_part(A)
    gate_stage(stages)

    @pl.when(leads)
    def _():
        def spread_end(k, c):
            await_bytes(gate_sums.at[stages], spread_send.at[k])
            return c

        lax.fori_loop(1, GROUP, spread_end, 0)

    @pl.when(not_(leads))
    def _():
        await_bytes(gate_own.at[pl.ds(0, 8)], gate_send.at[stages])
        await_bytes(gate_sums.at[stages], gate_recv.at[stages])

    heads = []
    for job, owners in ((A, ((0, 1), (2, 3))), (B, ((0, 3), (1, 2)))):
        part = slice(HERE[job], HERE[job] + HEADS[job])
        for one, two in owners:
            for side in range(2):
                both = gate_sums[stages, one * 2 + side] + gate_sums[stages, two * 2 + side]
                heads.append(both[part])
    gate_out_ref[...] = jnp.concatenate(heads, axis=0)

    await_bytes(media_buf.at[pl.ds(0, GROUP - 1)], media_send)
    for job in (A, B):
        for t in range(6):
            sent = lat_buf.at[pl.ds(0, 3), :, :, here(job)] if t == LATS else q_buf.at[pl.ds(0, 3 * ROWS), here(job)]
            await_bytes(sent, in_send.at[job, t])
            sent = glat_buf.at[pl.ds(0, 3), :, :, here(job)] if t == GLAT else out_buf.at[pl.ds(0, 3 * ROWS), here(job)]
            await_bytes(sent, out_send.at[job, t])
        await_bytes(lat_buf.at[pl.ds(0, 4), :, :, here(job)], pass_send.at[job, LATS])
        await_bytes(glat_buf.at[pl.ds(0, 4), :, :, here(job)], part_send.at[job, 2])

    def sent_rows(job, rows, pass_only, part_only):
        for t in (0, 1):
            if pass_only:
                await_bytes(k_buf.at[pl.ds(0, rows), here(job)], pass_send.at[job, t])
            if part_only:
                await_bytes(gk_buf.at[pl.ds(0, rows), here(job)], part_send.at[job, t])

    @pl.when(is_inner)
    def _():
        sent_rows(A, 2 * BLOCK, True, False)
        sent_rows(A, BLOCK, False, True)

    @pl.when(not_(is_inner))
    def _():
        sent_rows(A, BLOCK, True, False)
        sent_rows(A, 2 * BLOCK, False, True)

    pl.when(low)(lambda: sent_rows(B, 2 * BLOCK, True, False))
    pl.when(not_(low))(lambda: sent_rows(B, 2 * BLOCK, False, True))
    for t in range(6):
        await_bytes(out_refs[t], out_recv.at[t])


def finish_kernel(*refs):
    count = len(refs) // 2
    sems = refs[-1]
    copies = [pltpu.make_async_copy(refs[i], refs[count + i], sems.at[i]) for i in range(count)]
    for copy in copies:
        copy.start()
    for copy in copies:
        copy.wait()


def per_device(x_count, z_count, q, k, v, qc, lat, media, gate, cot):
    anywhere = pl.BlockSpec(memory_space=pl.ANY)
    vmem = pl.BlockSpec(memory_space=pltpu.VMEM)
    token = jax.ShapeDtypeStruct((1, ROWS, WIDTH), BF16)
    gate_shape = (ALL_HEADS, E)
    stages = (x_count * z_count).bit_length() - 1
    outs = (token,) * 5 + (jax.ShapeDtypeStruct(lat.shape, BF16), jax.ShapeDtypeStruct(gate_shape, F32))
    queries = pltpu.VMEM((2 * BLOCK, COLS), BF16)
    tokens = pltpu.VMEM((DOC, COLS), BF16)
    latents = pltpu.VMEM((GROUP, 2, LAT, COLS), BF16)
    dma = pltpu.SemaphoreType.DMA
    results = pl.pallas_call(
        functools.partial(kernel, x_count, z_count),
        name="attention",
        out_shape=outs,
        in_specs=[anywhere] * 8,
        out_specs=[anywhere] * 6 + [vmem],
        scratch_shapes=[
            queries, queries, queries, tokens, tokens, latents, pltpu.VMEM((GROUP, 1, ROWS), jnp.int32),
            queries, queries, queries, tokens, tokens, latents, tokens, tokens, latents,
            pltpu.VMEM((2 * BLOCK, COLS), F32), pltpu.VMEM((DOC, E), F32), pltpu.VMEM((DOC, E), F32),
            pltpu.VMEM((ALL_HEADS + 8, E), F32), pltpu.VMEM((16, E), F32), pltpu.VMEM((GROUP, 8, E), F32),
            pltpu.VMEM((stages + 1, GROUP, 8, E), F32), pltpu.VMEM((stages, GROUP, 8, E), F32),
            dma(()), dma(()), dma(()), dma((2, 6)), dma((2, 6)), dma((2, 3)), dma((2, 3)), dma((2, 3)), dma((2, 3)),
            dma((2, 6)), dma((6,)), dma((GROUP,)), dma((stages + 1,)), dma((stages + 1,)), dma((GROUP,)),
        ],
        compiler_params=pltpu.CompilerParams(
            collective_id=0, has_side_effects=True, vmem_limit_bytes=95 << 19
        ),
    )(q, k, v, qc, lat, cot, media, gate.reshape(gate_shape))
    done = pl.pallas_call(
        finish_kernel,
        name="finish",
        out_shape=outs,
        in_specs=[vmem] * 7,
        out_specs=[anywhere] * 7,
        scratch_shapes=[dma((7,))],
        compiler_params=pltpu.CompilerParams(vmem_limit_bytes=47 << 20),
    )(*results)
    return (*done[:6], done[6].reshape(WIDTH))


def solution(mesh):
    token = P("doc", "seq", None)
    latent = P("doc", "seq", None, None, None)
    return jax.shard_map(
        functools.partial(per_device, mesh.shape["seq"] // GROUP, mesh.shape["doc"]),
        mesh=mesh,
        in_specs=(token, token, token, token, latent, P("doc", "seq"), P(), token),
        out_specs=(token, token, token, token, token, latent, P()),
        check_vma=False,
    )
```
